512 devices in a mesh: ta: 16 (over z), gx: 32 (over y, x, core).
Axes of the slice: x: 4, y: 4, z: 16, core: 2. Of those that a mesh axis runs over, the one named last changes fastest.
Arguments:
- envelope: float32 [2, 512, 256, 256], P(None, 'ta', 'gx'), may hold values from -6 to 6
- density_map: float32 [256, 256], P('gx'), may hold values from 0.3 to 3
- disp_phase: float32 [512], replicated, may hold values from -3.140625 to 3.140625
Outputs:
- propagated: float32 [2, 512, 256, 256], P(None, 'ta', 'gx')
The draws below stay inside these ranges and needn't reach their ends.
All inputs are finite; a program needn't handle non-finite values.
Results may differ from the reference program's by a relative error of at most 0.0003.
Values sent between devices are 32-bit elements; how exact they have to be, the bound alone decides.
A program may use at most 64 MiB of HBM per device.

```python
import math
import jax
import jax.numpy as jnp

NT = 512
NY = 256
STEPS = 2
NX = 256


def level_of(stream_key, dims, shards, low, top_value):
    gain = 1.0
    for position, blocks in shards:
        heights = jax.random.uniform(jax.random.fold_in(jax.random.fold_in(stream_key, 6), position), (blocks,), jnp.float32, low / len(shards), top_value / len(shards))
        gain = gain * jnp.repeat(jnp.exp(heights), dims[position] // blocks).reshape((-1,) + (1,) * (len(dims) - 1 - position))
    return gain


def gaussian(rng, extent, deviation, bound, split=(), kind=jnp.bfloat16):
    entries = jax.random.normal(rng, extent, jnp.float32) * deviation
    if len(split) > 0:
        entries = level_of(rng, extent, split, -0.22, 0.18) * entries
    return jnp.clip(entries, min=-bound, max=bound).astype(kind)


def setup_inputs(seed: int = 0) -> dict:
    key_list = jax.random.split(jax.random.key(seed), 4)
    envelope = gaussian(key_list[0], (2, NT, NX, NY), 1.0, 6.0, ((1, 16), (2, 32)), jnp.float32)
    density_map = jnp.clip(jnp.exp(math.log(3.0) - 2.3025851 * jax.random.uniform(key_list[1], (NX, NY), jnp.float32) ** level_of(key_list[1], (NX, NY), ((0, 32),), -0.2, 0.2)), 0.3, 3.0)
    disp_phase = jnp.clip(jax.random.uniform(key_list[2], (NT,), jnp.float32, -3.140625, 3.140625), -3.140625, 3.140625)
    return dict(envelope=envelope, density_map=density_map, disp_phase=disp_phase)


diffract_step = 0.25
ionize_gain = 0.4
kerr_gain = 0.5
plasma_gain = 1.0
absorb_gain = 0.05


def laplace(values):
    padded = jnp.pad(values, ((0, 0), (1, 1), (1, 1)))
    return padded[:, 2:, 1:-1] + padded[:, :-2, 1:-1] + padded[:, 1:-1, 2:] + padded[:, 1:-1, :-2] - 4.0 * values


def diffract(real_part, imag_part):
    total_re, total_im = real_part, imag_part
    term_re, term_im = real_part, imag_part
    for number in range(1, 5):
        lap_re = laplace(term_re)
        lap_im = laplace(term_im)
        term_re, term_im = -diffract_step * lap_im / number, diffract_step * lap_re / number
        total_re = total_re + term_re
        total_im = total_im + term_im
    return total_re, total_im


def nonlinear(real_part, imag_part, density_map):
    intensity = real_part * real_part + imag_part * imag_part
    rate = density_map[None] * intensity * intensity * (ionize_gain / NT)
    plasma = jnp.cumsum(rate, axis=0) - rate
    phase = kerr_gain * intensity - plasma_gain * plasma
    amplitude = jnp.exp(-absorb_gain * plasma)
    cosine = jnp.cos(phase) * amplitude
    sine = jnp.sin(phase) * amplitude
    return real_part * cosine - imag_part * sine, real_part * sine + imag_part * cosine


def disperse(real_part, imag_part, disp_phase):
    spectrum = jnp.fft.fft(real_part + 1j * imag_part, axis=0)
    spectrum = spectrum * jnp.exp(1j * disp_phase)[:, None, None]
    back = jnp.fft.ifft(spectrum, axis=0)
    return jnp.real(back).astype(real_part.dtype), jnp.imag(back).astype(real_part.dtype)


def reference(envelope, density_map, disp_phase):
    real_part, imag_part = envelope[0], envelope[1]
    for number in range(STEPS):
        real_part, imag_part = diffract(real_part, imag_part)
        real_part, imag_part = nonlinear(real_part, imag_part, density_map)
        real_part, imag_part = disperse(real_part, imag_part, disp_phase)
    return jnp.stack([real_part, imag_part])
```

```python
import functools
import math

import jax
import jax.numpy as jnp
import ml_dtypes
import numpy as np
from jax import lax
from jax.experimental import pallas as pl
from jax.experimental.pallas import tpu as pltpu
from jax.sharding import PartitionSpec as P

MESH = pl.DeviceIdType.MESH
F32 = jnp.float32
BF16 = jnp.bfloat16

STEPS = 2
NT = 512
NZ = 16
TL = NT // NZ
NG = 32
XR = 8
NY = 256
YC = NY // NZ
CELLS = XR * YC
OWN = 2 * CELLS
HALO = 4
PAIR = 2 * YC

UP = OWN
DOWN = UP + HALO * PAIR
LEFT = DOWN + HALO * PAIR
RIGHT = LEFT + 8 * XR
CORNER = RIGHT + 8 * XR
EXT = CORNER + 4 * 24

diffract_step = 0.25
ionize_gain = 0.4
kerr_gain = 0.5
plasma_gain = 1.0
absorb_gain = 0.05


def row_cells():
    rows = []
    for x in range(XR):
        for c in range(2):
            for y in range(YC):
                rows.append((x, y, c))
    for base in (-HALO, XR):
        for x in range(HALO):
            for c in range(2):
                for y in range(YC):
                    rows.append((base + x, y, c))
    for base in (-HALO, YC):
        for x in range(XR):
            for c in range(2):
                for y in range(HALO):
                    rows.append((x, base + y, c))
    for xbase in (-3, XR):
        for ybase in (-HALO, YC):
            for x in range(3):
                for c in range(2):
                    for y in range(HALO):
                        rows.append((xbase + x, ybase + y, c))
    return rows


def diffraction_matrices():
    rows = row_cells()
    wide, high = YC + 2 * HALO, XR + 2 * HALO
    result = np.zeros((9, 2, OWN, EXT), ml_dtypes.bfloat16)
    for vx in range(3):
        for vy in range(3):
            inside = np.ones((high, wide), bool)
            if vx == 0:
                inside[:HALO] = False
            if vx == 2:
                inside[-HALO:] = False
            if vy == 0:
                inside[:, :HALO] = False
            if vy == 2:
                inside[:, -HALO:] = False
            count = high * wide
            lap = np.zeros((count, count))
            for x in range(high):
                for y in range(wide):
                    if not inside[x, y]:
                        continue
                    lap[x * wide + y, x * wide + y] = -4.0
                    for dx, dy in ((1, 0), (-1, 0), (0, 1), (0, -1)):
                        a, b = x + dx, y + dy
                        if 0 <= a < high and 0 <= b < wide and inside[a, b]:
                            lap[x * wide + y, a * wide + b] = 1.0
            own = [(x + HALO) * wide + y + HALO for x in range(XR) for y in range(YC)]
            power = np.eye(count)[own].astype(complex)
            total = power.copy()
            for n in range(1, 5):
                power = power @ lap * (1j * diffract_step / n)
                total = total + power
            place = {(x, y): i for i, (x, y) in enumerate((x, y) for x in range(XR) for y in range(YC))}
            matrix = np.zeros((OWN, EXT))
            for out_row, (x, y, c) in enumerate(rows[:OWN]):
                line = total[place[(x, y)]]
                for col, (a, b, d) in enumerate(rows):
                    value = line[(a + HALO) * wide + b + HALO]
                    if c == d:
                        matrix[out_row, col] = value.real
                    else:
                        matrix[out_row, col] = -value.imag if c == 0 else value.imag
            matrix = matrix.astype(np.float32)
            upper = matrix.astype(ml_dtypes.bfloat16)
            result[vx * 3 + vy, 0] = upper
            result[vx * 3 + vy, 1] = (matrix - upper.astype(np.float32)).astype(ml_dtypes.bfloat16)
    return result


def fourier_matrices():
    index = np.arange(NT)
    angles = (index[:, None] * index[None, :] % NT) * (2.0 * math.pi / NT)
    return np.stack([np.cos(angles), np.sin(angles)]).astype(np.float32)


def split(value):
    upper = value.astype(BF16)
    return upper, (value - upper.astype(F32)).astype(BF16)


def dot(a, b):
    return jnp.dot(a, b, preferred_element_type=F32)


def triple(ah, al, bh, bl):
    return dot(ah, bh) + dot(ah, bl) + dot(al, bh)


def sincos(angle):
    turns = jnp.floor(angle * (2.0 / math.pi) + 0.5)
    rest = ((angle - turns * 1.5703125) - turns * 4.837512969970703125e-4) - turns * 7.54978995489188216e-8
    quarter = turns.astype(jnp.int32)
    z = rest * rest
    sine = ((-1.9515295891e-4 * z + 8.3321608736e-3) * z - 1.6666654611e-1) * (z * rest) + rest
    cosine = ((2.443315711809948e-5 * z - 1.388731625493765e-3) * z + 4.166664568298827e-2) * (z * z) + (1.0 - 0.5 * z)
    odd = (quarter & 1) == 1
    a = jnp.where(odd, cosine, sine)
    b = jnp.where(odd, sine, cosine)
    a = jnp.where((quarter & 2) == 2, -a, a)
    b = jnp.where(((quarter + 1) & 2) == 2, -b, b)
    return a, b


def kernel(
    env, dens, phase, wmat, fourier, out,
    stage, sbuf, rbuf, ext, exth, extl, ylo, yhi, ch, cl, tri, wbuf, fbuf, dcol,
    grid, inten, rh, rl, plasma, uh, ul, spec, fin, obuf,
    local_sem, asend, arecv, hsend, hrecv, bsend, brecv,
):
    me = lax.axis_index("ta")
    gx = lax.axis_index("gx")

    loads = [
        pltpu.make_async_copy(env.at[:, pl.ds(h * 128, 128)], stage.at[h], local_sem.at[4 + h]) for h in range(2)
    ]
    for load in loads:
        load.start()
    variant = (lax.div(gx + NG - 2, NG - 1) + lax.div(gx, NG - 1)) * 3 + lax.div(me + NZ - 2, NZ - 1) + lax.div(me, NZ - 1)
    load_w = pltpu.make_async_copy(wmat.at[variant], wbuf, local_sem.at[1])
    load_w.start()
    load_f = pltpu.make_async_copy(fourier, fbuf, local_sem.at[2])
    load_f.start()

    def ring(step):
        return lax.rem(me + step + NZ, NZ)

    def side(step):
        return lax.rem(gx + step + NG, NG)

    barrier = pltpu.get_barrier_semaphore()
    for step in range(1, NZ):
        pl.semaphore_signal(barrier, inc=1, device_id=(ring(step), gx), device_id_type=MESH)
    for dx in (-1, 1):
        for dz in (-1, 0, 1):
            pl.semaphore_signal(barrier, inc=1, device_id=(ring(dz), side(dx)), device_id_type=MESH)

    for load in loads:
        load.wait()
    slot = lax.broadcasted_iota(jnp.int32, (2 * TL, 128), 1) // YC
    for h in range(2):
        turned = []
        for x in range(XR):
            part = stage[h, pl.ds(x, 2 * TL, stride=XR), :]
            turned.append(pltpu.roll(part, YC * x, axis=1) if x else part)
        for jj in range(8):
            piece = turned[0]
            for x in range(1, XR):
                piece = jnp.where(slot == (jj + x) % 8, turned[x], piece)
            if jj:
                piece = pltpu.roll(piece, 128 - YC * jj, axis=1)
            sbuf[h * 8 + jj] = piece.reshape(2, TL, 128)

    pl.semaphore_wait(barrier, NZ - 1 + 6)

    def column_copy(step):
        peer = ring(step)
        return pltpu.make_async_remote_copy(
            src_ref=sbuf.at[peer],
            dst_ref=rbuf.at[:, pl.ds(pl.multiple_of(me * TL, TL), TL), :],
            send_sem=asend.at[step],
            recv_sem=arecv.at[step],
            device_id=(peer, gx),
            device_id_type=MESH,
        )

    order = [s for k in range(8, 0, -1) for s in ((k, NZ - k) if k < 8 else (8,))]
    for step in order:
        column_copy(step).start()
    mine = pltpu.make_async_copy(
        sbuf.at[me], rbuf.at[:, pl.ds(pl.multiple_of(me * TL, TL), TL), :], local_sem.at[3]
    )
    mine.start()

    load_f.wait()
    turn = phase[...]
    sine, cosine = sincos(turn)
    pair = jnp.concatenate([cosine, sine] * 4, axis=0) * (1.0 / NT)
    by_cos = jnp.dot(pair, fbuf[0], precision=lax.Precision.HIGHEST, preferred_element_type=F32)
    by_sin = jnp.dot(pair, fbuf[1], precision=lax.Precision.HIGHEST, preferred_element_type=F32)
    rows16 = lax.broadcasted_iota(jnp.int32, (16, NT), 0)
    for part, line in enumerate((by_cos[0:1] - by_sin[1:2], by_sin[0:1] + by_cos[1:2])):
        base = jnp.broadcast_to(line, (16, NT))
        for bit in range(4):
            base = jnp.where((rows16 >> bit) & 1 == 1, pltpu.roll(base, 1 << bit, axis=1), base)
        for block in range(NT // 16):
            high, low = split(pltpu.roll(base, 16 * block, axis=1) if block else base)
            ch[16 * block : 16 * block + 16, part * NT : (part + 1) * NT] = high
            cl[16 * block : 16 * block + 16, part * NT : (part + 1) * NT] = low

    def tri_rows(block, carry):
        first = pl.multiple_of(block * 16, 16)
        row = lax.broadcasted_iota(jnp.int32, (16, NT), 0) + first
        col = lax.broadcasted_iota(jnp.int32, (16, NT), 1)
        tri[pl.ds(first, 16), :] = jnp.where(row < col, 1.0, 0.0).astype(BF16)
        return carry

    lax.fori_loop(0, NT // 16, tri_rows, 0)
    lane = lax.broadcasted_iota(jnp.int32, (YC, NY), 1)
    row = lax.broadcasted_iota(jnp.int32, (YC, NY), 0)
    wanted = lane == row + me * YC
    for x in range(XR):
        line = jnp.broadcast_to(dens[x : x + 1, :], (YC, NY))
        column = jnp.sum(jnp.where(wanted, line, 0.0), axis=1, keepdims=True)
        dcol[x * YC : (x + 1) * YC, :] = jnp.broadcast_to(column * (ionize_gain / NT), (YC, NT))
    load_w.wait()

    mine.wait()
    for step in order:
        column_copy(step).wait_recv()
    for c in range(2):
        turned = rbuf[c].T
        for x in range(XR):
            ext[0, x * PAIR + c * YC : x * PAIR + (c + 1) * YC, :] = turned[x * YC : (x + 1) * YC]

    low4 = lax.broadcasted_iota(jnp.int32, (8, NT), 0) < HALO

    for number in range(STEPS):
        tile = ext.at[number]
        lo, hi = ylo.at[number], yhi.at[number]

        def halo_copy(index, source, first, dx, dz):
            return pltpu.make_async_remote_copy(
                src_ref=source,
                dst_ref=tile.at[pl.ds(first, source.shape[0]), :],
                send_sem=hsend.at[number, index],
                recv_sem=hrecv.at[number, index],
                device_id=(ring(dz), side(dx)),
                device_id_type=MESH,
            )

        copies = [
            halo_copy(0, tile.at[pl.ds(HALO * PAIR, HALO * PAIR), :], UP, 1, 0),
            halo_copy(1, tile.at[pl.ds(0, HALO * PAIR), :], DOWN, -1, 0),
            halo_copy(2, hi, LEFT, 0, 1),
            halo_copy(3, lo, RIGHT, 0, -1),
            halo_copy(4, hi.at[pl.ds(40, 24), :], CORNER, 1, 1),
            halo_copy(5, lo.at[pl.ds(40, 24), :], CORNER + 24, 1, -1),
            halo_copy(6, hi.at[pl.ds(0, 24), :], CORNER + 48, -1, 1),
            halo_copy(7, lo.at[pl.ds(0, 24), :], CORNER + 72, -1, -1),
        ]
        copies[0].start()
        copies[1].start()
        for x in range(XR):
            first = x * PAIR
            lo[8 * x : 8 * x + 8, :] = jnp.where(
                low4, tile[first : first + 8, :], pltpu.roll(tile[first + 16 : first + 24, :], 4, axis=0)
            )
            hi[8 * x : 8 * x + 8, :] = jnp.where(
                low4, pltpu.roll(tile[first + 8 : first + 16, :], 4, axis=0), tile[first + 24 : first + 32, :]
            )
        for copy in copies[2:]:
            copy.start()

        def split_rows(block, carry):
            place = pl.ds(pl.multiple_of(block * 32, 32), 32)
            high, low = split(tile[place, :])
            exth[place, :] = high
            extl[place, :] = low
            return carry

        lax.fori_loop(0, OWN // 32, split_rows, 0)
        grid[...] = triple(wbuf[0, :, :OWN], wbuf[1, :, :OWN], exth[:OWN], extl[:OWN])
        for copy in copies:
            copy.wait_recv()
        lax.fori_loop(OWN // 32, EXT // 32, split_rows, 0)
        grid[...] += triple(wbuf[0, :, OWN:], wbuf[1, :, OWN:], exth[OWN:], extl[OWN:])

        def rates(x, carry):
            first = pl.multiple_of(x * PAIR, PAIR)
            place = pl.ds(pl.multiple_of(x * YC, YC), YC)
            re = grid[pl.ds(first, YC), :]
            im = grid[pl.ds(first + YC, YC), :]
            intensity = re * re + im * im
            inten[place, :] = intensity
            high, low = split(dcol[place, :] * intensity * intensity)
            rh[place, :] = high
            rl[place, :] = low
            return carry

        lax.fori_loop(0, XR, rates, 0)
        plasma[...] = dot(rh[...], tri[...]) + dot(rl[...], tri[...])

        def kick(x, carry):
            first = pl.multiple_of(x * PAIR, PAIR)
            place = pl.ds(pl.multiple_of(x * YC, YC), YC)
            re = grid[pl.ds(first, YC), :]
            im = grid[pl.ds(first + YC, YC), :]
            earlier = plasma[place, :]
            sine, cosine = sincos(kerr_gain * inten[place, :] - plasma_gain * earlier)
            amplitude = jnp.exp(-absorb_gain * earlier)
            sine = sine * amplitude
            cosine = cosine * amplitude
            high, low = split(re * cosine - im * sine)
            uh[pl.ds(first, YC), :] = high
            ul[pl.ds(first, YC), :] = low
            high, low = split(re * sine + im * cosine)
            uh[pl.ds(first + YC, YC), :] = high
            ul[pl.ds(first + YC, YC), :] = low
            return carry

        lax.fori_loop(0, XR, kick, 0)
        spec[...] = triple(uh[...], ul[...], ch[...], cl[...])
        if number + 1 < STEPS:
            for x in range(XR):
                first = x * PAIR
                re = spec[first : first + YC, :]
                im = spec[first + YC : first + PAIR, :]
                ext[number + 1, first : first + YC, :] = re[:, :NT] - im[:, NT:]
                ext[number + 1, first + YC : first + PAIR, :] = re[:, NT:] + im[:, :NT]
        else:
            res, ims = [], []
            for x in range(XR):
                first = x * PAIR
                re = spec[first : first + YC, :]
                im = spec[first + YC : first + PAIR, :]
                res.append(re[:, :NT] - im[:, NT:])
                ims.append(re[:, NT:] + im[:, :NT])
            fin[0] = jnp.concatenate(res, axis=0).T
            fin[1] = jnp.concatenate(ims, axis=0).T
        for copy in copies:
            copy.wait_send()

    def shard_copy(step):
        peer = ring(step)
        return pltpu.make_async_remote_copy(
            src_ref=fin.at[:, pl.ds(pl.multiple_of(peer * TL, TL), TL), :],
            dst_ref=obuf.at[me],
            send_sem=bsend.at[step],
            recv_sem=brecv.at[step],
            device_id=(peer, gx),
            device_id_type=MESH,
        )

    for step in order:
        shard_copy(step).start()
    mine = pltpu.make_async_copy(
        fin.at[:, pl.ds(pl.multiple_of(me * TL, TL), TL), :], obuf.at[me], local_sem.at[3]
    )
    mine.start()
    for step in order:
        column_copy(step).wait_send()
    mine.wait()
    for step in order:
        shard_copy(step).wait_recv()
    stores = [
        pltpu.make_async_copy(stage.at[h], out.at[:, pl.ds(h * 128, 128)], local_sem.at[4 + h]) for h in range(2)
    ]
    for h in range(2):
        turned = []
        for jj in range(8):
            part = obuf[h * 8 + jj].reshape(2 * TL, 128)
            turned.append(pltpu.roll(part, YC * jj, axis=1) if jj else part)
        for x in range(XR):
            piece = turned[0]
            for jj in range(1, 8):
                piece = jnp.where(slot == (jj + x) % 8, turned[jj], piece)
            if x:
                piece = pltpu.roll(piece, 128 - YC * x, axis=1)
            stage[h, pl.ds(x, 2 * TL, stride=XR), :] = piece
        stores[h].start()
    for step in order:
        shard_copy(step).wait_send()
    for store in stores:
        store.wait()


def per_device(envelope, density_map, disp_phase):
    rows = 2 * TL * XR
    vmem = pl.BlockSpec(memory_space=pltpu.VMEM)
    anywhere = pl.BlockSpec(memory_space=pl.ANY)
    dma = pltpu.SemaphoreType.DMA
    result = pl.pallas_call(
        kernel,
        out_shape=jax.ShapeDtypeStruct((rows, NY), F32),
        in_specs=[anywhere, vmem, vmem, anywhere, anywhere],
        out_specs=anywhere,
        scratch_shapes=[
            pltpu.VMEM((2, rows, 128), F32),
            pltpu.VMEM((NZ, 2, TL, 128), F32),
            pltpu.VMEM((2, NT, CELLS), F32),
            pltpu.VMEM((STEPS, EXT, NT), F32),
            pltpu.VMEM((EXT, NT), BF16),
            pltpu.VMEM((EXT, NT), BF16),
            pltpu.VMEM((STEPS, 8 * XR, NT), F32),
            pltpu.VMEM((STEPS, 8 * XR, NT), F32),
            pltpu.VMEM((NT, 2 * NT), BF16),
            pltpu.VMEM((NT, 2 * NT), BF16),
            pltpu.VMEM((NT, NT), BF16),
            pltpu.VMEM((2, OWN, EXT), BF16),
            pltpu.VMEM((2, NT, NT), F32),
            pltpu.VMEM((CELLS, NT), F32),
            pltpu.VMEM((OWN, NT), F32),
            pltpu.VMEM((CELLS, NT), F32),
            pltpu.VMEM((CELLS, NT), BF16),
            pltpu.VMEM((CELLS, NT), BF16),
            pltpu.VMEM((CELLS, NT), F32),
            pltpu.VMEM((OWN, NT), BF16),
            pltpu.VMEM((OWN, NT), BF16),
            pltpu.VMEM((OWN, 2 * NT), F32),
            pltpu.VMEM((2, NT, CELLS), F32),
            pltpu.VMEM((NZ, 2, TL, 128), F32),
            dma((6,)),
            dma((NZ,)),
            dma((NZ,)),
            dma((STEPS, 8)),
            dma((STEPS, 8)),
            dma((NZ,)),
            dma((NZ,)),
        ],
        compiler_params=pltpu.CompilerParams(
            collective_id=0, has_side_effects=True, vmem_limit_bytes=48 * 1024 * 1024
        ),
        name="filament",
    )(
        envelope.reshape(rows, NY),
        density_map,
        disp_phase.reshape(1, NT),
        jnp.asarray(diffraction_matrices()),
        jnp.asarray(fourier_matrices()),
    )
    return result.reshape(2, TL, XR, NY)


def solution(mesh):
    placed = (P(None, "ta", "gx", None), P("gx", None), P())
    return jax.shard_map(
        per_device, mesh=mesh, in_specs=placed, out_specs=P(None, "ta", "gx", None), check_vma=False
    )
```

```python
import functools
import math

import jax
import jax.numpy as jnp
import ml_dtypes
import numpy as np
from jax import lax
from jax.experimental import pallas as pl
from jax.experimental.pallas import tpu as pltpu
from jax.sharding import PartitionSpec as P

MESH = pl.DeviceIdType.MESH
F32 = jnp.float32
BF16 = jnp.bfloat16

STEPS = 2
NT = 512
NZ = 16
TL = NT // NZ
NG = 32
XR = 8
NY = 256
YC = NY // NZ
CELLS = XR * YC
OWN = 2 * CELLS
HALO = 4
TC = 8
PAIR = 2 * YC

UP = OWN
DOWN = UP + HALO * PAIR
LEFT = DOWN + HALO * PAIR
RIGHT = LEFT + 8 * XR
CORNER = RIGHT + 8 * XR
EXT = CORNER + 4 * 24

diffract_step = 0.25
ionize_gain = 0.4
kerr_gain = 0.5
plasma_gain = 1.0
absorb_gain = 0.05


def row_cells():
    rows = []
    for x in range(XR):
        for c in range(2):
            for y in range(YC):
                rows.append((x, y, c))
    for base in (-HALO, XR):
        for x in range(HALO):
            for c in range(2):
                for y in range(YC):
                    rows.append((base + x, y, c))
    for base in (-HALO, YC):
        for x in range(XR):
            for c in range(2):
                for y in range(HALO):
                    rows.append((x, base + y, c))
    for xbase in (-3, XR):
        for ybase in (-HALO, YC):
            for x in range(3):
                for c in range(2):
                    for y in range(HALO):
                        rows.append((xbase + x, ybase + y, c))
    return rows


def diffraction_matrices():
    rows = row_cells()
    wide, high = YC + 2 * HALO, XR + 2 * HALO
    result = np.zeros((9, 2, OWN, EXT), ml_dtypes.bfloat16)
    for vx in range(3):
        for vy in range(3):
            inside = np.ones((high, wide), bool)
            if vx == 0:
                inside[:HALO] = False
            if vx == 2:
                inside[-HALO:] = False
            if vy == 0:
                inside[:, :HALO] = False
            if vy == 2:
                inside[:, -HALO:] = False
            count = high * wide
            lap = np.zeros((count, count))
            for x in range(high):
                for y in range(wide):
                    if not inside[x, y]:
                        continue
                    lap[x * wide + y, x * wide + y] = -4.0
                    for dx, dy in ((1, 0), (-1, 0), (0, 1), (0, -1)):
                        a, b = x + dx, y + dy
                        if 0 <= a < high and 0 <= b < wide and inside[a, b]:
                            lap[x * wide + y, a * wide + b] = 1.0
            own = [(x + HALO) * wide + y + HALO for x in range(XR) for y in range(YC)]
            power = np.eye(count)[own].astype(complex)
            total = power.copy()
            for n in range(1, 5):
                power = power @ lap * (1j * diffract_step / n)
                total = total + power
            place = {(x, y): i for i, (x, y) in enumerate((x, y) for x in range(XR) for y in range(YC))}
            matrix = np.zeros((OWN, EXT))
            for out_row, (x, y, c) in enumerate(rows[:OWN]):
                line = total[place[(x, y)]]
                for col, (a, b, d) in enumerate(rows):
                    value = line[(a + HALO) * wide + b + HALO]
                    if c == d:
                        matrix[out_row, col] = value.real
                    else:
                        matrix[out_row, col] = -value.imag if c == 0 else value.imag
            matrix = matrix.astype(np.float32)
            upper = matrix.astype(ml_dtypes.bfloat16)
            result[vx * 3 + vy, 0] = upper
            result[vx * 3 + vy, 1] = (matrix - upper.astype(np.float32)).astype(ml_dtypes.bfloat16)
    return result


def fourier_matrices():
    index = np.arange(NT)
    angles = (index[:, None] * index[None, :] % NT) * (2.0 * math.pi / NT)
    return np.stack([np.cos(angles), np.sin(angles)]).astype(np.float32)


def split(value):
    upper = value.astype(BF16)
    return upper, (value - upper.astype(F32)).astype(BF16)


def dot(a, b):
    return jnp.dot(a, b, preferred_element_type=F32)


def triple(ah, al, bh, bl):
    return dot(ah, bh) + dot(ah, bl) + dot(al, bh)


def sincos(angle):
    turns = jnp.floor(angle * (2.0 / math.pi) + 0.5)
    rest = ((angle - turns * 1.5703125) - turns * 4.837512969970703125e-4) - turns * 7.54978995489188216e-8
    quarter = turns.astype(jnp.int32)
    z = rest * rest
    sine = ((-1.9515295891e-4 * z + 8.3321608736e-3) * z - 1.6666654611e-1) * (z * rest) + rest
    cosine = ((2.443315711809948e-5 * z - 1.388731625493765e-3) * z + 4.166664568298827e-2) * (z * z) + (1.0 - 0.5 * z)
    odd = (quarter & 1) == 1
    a = jnp.where(odd, cosine, sine)
    b = jnp.where(odd, sine, cosine)
    a = jnp.where((quarter & 2) == 2, -a, a)
    b = jnp.where(((quarter + 1) & 2) == 2, -b, b)
    return a, b


def diffract(re, im, above, below, lane):
    edge = HALO * TC
    total_re, total_im = re[edge:-edge], im[edge:-edge]
    for number in range(1, HALO + 1):
        terms = []
        for part in (re, im):
            centre = part[TC:-TC]
            left = jnp.where(lane[: centre.shape[0]] == 0, 0.0, pltpu.roll(centre, 1, axis=1))
            right = jnp.where(lane[: centre.shape[0]] == NY - 1, 0.0, pltpu.roll(centre, NY - 1, axis=1))
            lapped = (part[2 * TC :] + part[: -2 * TC]) + (left + right) - 4.0 * centre
            lapped = lapped * (diffract_step / number)
            rest = (HALO - number) * TC
            if rest:
                lapped = jnp.concatenate([lapped[:rest] * above, lapped[rest:-rest], lapped[-rest:] * below], axis=0)
            terms.append(lapped)
        re, im = -terms[1], terms[0]
        rest = (HALO - number) * TC
        total_re = total_re + (re[rest:-rest] if rest else re)
        total_im = total_im + (im[rest:-rest] if rest else im)
    return total_re, total_im


def kernel(
    env, dens, phase, wmat, fourier, out,
    stage, field, sbuf, rbuf, ext, exth, extl, ylo, yhi, ch, cl, tri, wbuf, fbuf, dcol,
    grid, inten, rh, rl, plasma, uh, ul, spec, fin, obuf,
    local_sem, xsend, xrecv, asend, arecv, hsend, hrecv, bsend, brecv,
):
    me = lax.axis_index("ta")
    gx = lax.axis_index("gx")

    loads = [
        pltpu.make_async_copy(env.at[:, pl.ds(h * 128, 128)], stage.at[h], local_sem.at[4 + h]) for h in range(2)
    ]
    for load in loads:
        load.start()
    variant = (lax.div(gx + NG - 2, NG - 1) + lax.div(gx, NG - 1)) * 3 + lax.div(me + NZ - 2, NZ - 1) + lax.div(me, NZ - 1)
    load_w = pltpu.make_async_copy(wmat.at[variant], wbuf, local_sem.at[2])
    load_w.start()
    load_f = pltpu.make_async_copy(fourier, fbuf, local_sem.at[3])
    load_f.start()

    def ring(step):
        return lax.rem(me + step + NZ, NZ)

    def side(step):
        return lax.rem(gx + step + NG, NG)

    barrier = pltpu.get_barrier_semaphore()
    for step in range(1, NZ):
        pl.semaphore_signal(barrier, inc=1, device_id=(ring(step), gx), device_id_type=MESH)
    for dx in (-1, 1):
        for dz in (-1, 0, 1):
            pl.semaphore_signal(barrier, inc=1, device_id=(ring(dz), side(dx)), device_id_type=MESH)

    for load in loads:
        load.wait()
    for h in range(2):
        for c in range(2):
            for x in range(XR):
                field[HALO + x, c, :, h * 128 : (h + 1) * 128] = stage[h, pl.ds(c * TL * XR + x, TL, stride=XR), :]

    pl.semaphore_wait(barrier, NZ - 1 + 6)

    def row_copies(q):
        times = pl.ds(pl.multiple_of(q * TC, TC), TC)
        return [
            pltpu.make_async_remote_copy(
                src_ref=field.at[pl.ds(source, HALO), :, times, :],
                dst_ref=field.at[pl.ds(target, HALO), :, times, :],
                send_sem=xsend.at[q, way],
                recv_sem=xrecv.at[q, way],
                device_id=(me, side(dx)),
                device_id_type=MESH,
            )
            for way, (source, target, dx) in enumerate(((XR, 0, 1), (HALO, HALO + XR, -1)))
        ]

    for q in range(TL // TC):
        for copy in row_copies(q):
            copy.start()

    def column_copy(group, index, step, first, count):
        peer = ring(step)
        return pltpu.make_async_remote_copy(
            src_ref=sbuf.at[group, peer, pl.ds(first, count), :],
            dst_ref=rbuf.at[group, pl.ds(pl.multiple_of(me * TL, TL) + first, count), :],
            send_sem=asend.at[index, step],
            recv_sem=arecv.at[index, step],
            device_id=(peer, gx),
            device_id_type=MESH,
        )

    order = [s for k in range(8, 0, -1) for s in ((k, NZ - k) if k < 8 else (8,))]
    messages = ((0, 0, 0, TL // 2), (0, 1, TL // 2, TL // 2), (1, 2, 0, TL))
    above = jnp.where(gx == 0, 0.0, 1.0).astype(F32)
    below = jnp.where(gx == NG - 1, 0.0, 1.0).astype(F32)

    def first_diffraction(q, carry):
        times = pl.ds(pl.multiple_of(q * TC, TC), TC)
        for copy in row_copies(q):
            copy.wait_recv()
        lane = lax.broadcasted_iota(jnp.int32, ((XR + 2 * HALO) * TC, NY), 1)
        slot = lax.broadcasted_iota(jnp.int32, (TC, 128), 1) // YC
        parts = []
        for c in range(2):
            value = field[:, c, times, :]
            value = jnp.concatenate([value[:HALO] * above, value[HALO:-HALO], value[-HALO:] * below], axis=0)
            parts.append(value.reshape((XR + 2 * HALO) * TC, NY))
        parts = diffract(parts[0], parts[1], above, below, lane)
        for h in range(2):
            for group in range(2):
                turned = []
                for s in range(8):
                    first = (group * HALO + s // 2) * TC
                    part = parts[s % 2][first : first + TC, h * 128 : (h + 1) * 128]
                    turned.append(pltpu.roll(part, YC * s, axis=1) if s else part)
                for jj in range(8):
                    piece = turned[0]
                    for s in range(1, 8):
                        piece = jnp.where(slot == (jj + s) % 8, turned[s], piece)
                    if jj:
                        piece = pltpu.roll(piece, 128 - YC * jj, axis=1)
                    sbuf[group, h * 8 + jj, times, :] = piece
        return carry

    half = TL // TC // 2
    lax.fori_loop(0, half, first_diffraction, 0)
    for step in order:
        column_copy(*messages[0][:2], step, *messages[0][2:]).start()
    lax.fori_loop(half, 2 * half, first_diffraction, 0)
    for group, index, first, count in messages[1:]:
        for step in order:
            column_copy(group, index, step, first, count).start()
    mine = [
        pltpu.make_async_copy(
            sbuf.at[group, me], rbuf.at[group, pl.ds(pl.multiple_of(me * TL, TL), TL), :], local_sem.at[group]
        )
        for group in range(2)
    ]
    for copy in mine:
        copy.start()

    load_f.wait()
    turn = phase[...]
    sine, cosine = sincos(turn)
    pair = jnp.concatenate([cosine, sine] * 4, axis=0) * (1.0 / NT)
    by_cos = jnp.dot(pair, fbuf[0], precision=lax.Precision.HIGHEST, preferred_element_type=F32)
    by_sin = jnp.dot(pair, fbuf[1], precision=lax.Precision.HIGHEST, preferred_element_type=F32)
    rows16 = lax.broadcasted_iota(jnp.int32, (16, NT), 0)
    for part, line in enumerate((by_cos[0:1] - by_sin[1:2], by_sin[0:1] + by_cos[1:2])):
        base = jnp.broadcast_to(line, (16, NT))
        for bit in range(4):
            base = jnp.where((rows16 >> bit) & 1 == 1, pltpu.roll(base, 1 << bit, axis=1), base)
        for block in range(NT // 16):
            high, low = split(pltpu.roll(base, 16 * block, axis=1) if block else base)
            ch[16 * block : 16 * block + 16, part * NT : (part + 1) * NT] = high
            cl[16 * block : 16 * block + 16, part * NT : (part + 1) * NT] = low

    def tri_rows(block, carry):
        first = pl.multiple_of(block * 16, 16)
        row = lax.broadcasted_iota(jnp.int32, (16, NT), 0) + first
        col = lax.broadcasted_iota(jnp.int32, (16, NT), 1)
        tri[pl.ds(first, 16), :] = jnp.where(row < col, 1.0, 0.0).astype(BF16)
        return carry

    lax.fori_loop(0, NT // 16, tri_rows, 0)
    lane = lax.broadcasted_iota(jnp.int32, (YC, NY), 1)
    row = lax.broadcasted_iota(jnp.int32, (YC, NY), 0)
    wanted = lane == row + me * YC
    for x in range(XR):
        line = jnp.broadcast_to(dens[x : x + 1, :], (YC, NY))
        column = jnp.sum(jnp.where(wanted, line, 0.0), axis=1, keepdims=True)
        dcol[x * YC : (x + 1) * YC, :] = jnp.broadcast_to(column * (ionize_gain / NT), (YC, NT))
    load_w.wait()

    def kick(group):
        def rates(x, carry):
            first = pl.multiple_of(x * PAIR, PAIR)
            place = pl.ds(pl.multiple_of(x * YC, YC), YC)
            re = grid[pl.ds(first, YC), :]
            im = grid[pl.ds(first + YC, YC), :]
            intensity = re * re + im * im
            inten[place, :] = intensity
            high, low = split(dcol[place, :] * intensity * intensity)
            rh[place, :] = high
            rl[place, :] = low
            return carry

        lax.fori_loop(group * HALO, (group + 1) * HALO, rates, 0)
        cells = slice(group * CELLS // 2, (group + 1) * CELLS // 2)
        plasma[cells, :] = dot(rh[cells, :], tri[...]) + dot(rl[cells, :], tri[...])

        def turn(x, carry):
            first = pl.multiple_of(x * PAIR, PAIR)
            place = pl.ds(pl.multiple_of(x * YC, YC), YC)
            re = grid[pl.ds(first, YC), :]
            im = grid[pl.ds(first + YC, YC), :]
            earlier = plasma[place, :]
            sine, cosine = sincos(kerr_gain * inten[place, :] - plasma_gain * earlier)
            amplitude = jnp.exp(-absorb_gain * earlier)
            sine = sine * amplitude
            cosine = cosine * amplitude
            high, low = split(re * cosine - im * sine)
            uh[pl.ds(first, YC), :] = high
            ul[pl.ds(first, YC), :] = low
            high, low = split(re * sine + im * cosine)
            uh[pl.ds(first + YC, YC), :] = high
            ul[pl.ds(first + YC, YC), :] = low
            return carry

        lax.fori_loop(group * HALO, (group + 1) * HALO, turn, 0)

    def disperse(group):
        rows = slice(group * OWN // 2, (group + 1) * OWN // 2)
        spec[rows, :] = triple(uh[rows, :], ul[rows, :], ch[...], cl[...])
        result = []
        for x in range(group * HALO, (group + 1) * HALO):
            re = spec[x * PAIR : x * PAIR + YC, :]
            im = spec[x * PAIR + YC : (x + 1) * PAIR, :]
            result.append(re[:, :NT] - im[:, NT:])
            result.append(re[:, NT:] + im[:, :NT])
        return result

    def halo_copy(index, source, first, dx, dz):
        return pltpu.make_async_remote_copy(
            src_ref=source,
            dst_ref=ext.at[pl.ds(first, source.shape[0]), :],
            send_sem=hsend.at[index],
            recv_sem=hrecv.at[index],
            device_id=(ring(dz), side(dx)),
            device_id_type=MESH,
        )

    def halo_copies(group):
        rows = pl.ds(group * 32, 32)
        towards = 2 * group - 1
        end = pl.ds(40 * group, 24)
        return [
            halo_copy(5 * group, ext.at[pl.ds(group * OWN // 2, OWN // 2), :], UP if group else DOWN, towards, 0),
            halo_copy(5 * group + 1, yhi.at[rows, :], LEFT + 32 * group, 0, 1),
            halo_copy(5 * group + 2, ylo.at[rows, :], RIGHT + 32 * group, 0, -1),
            halo_copy(5 * group + 3, yhi.at[end, :], CORNER + 48 * (1 - group), towards, 1),
            halo_copy(5 * group + 4, ylo.at[end, :], CORNER + 48 * (1 - group) + 24, towards, -1),
        ]

    def split_rows(block, carry):
        place = pl.ds(pl.multiple_of(block * 32, 32), 32)
        high, low = split(ext[place, :])
        exth[place, :] = high
        extl[place, :] = low
        return carry

    low4 = lax.broadcasted_iota(jnp.int32, (8, NT), 0) < HALO
    for group in range(2):
        mine[group].wait()
        for g, index, first, count in messages:
            if g == group:
                for step in order:
                    column_copy(g, index, step, first, count).wait_recv()
        base = group * OWN // 2
        grid[base : base + OWN // 2, :] = rbuf[group].T
        kick(group)
        result = disperse(group)
        for i, block in enumerate(result):
            ext[base + i * YC : base + (i + 1) * YC, :] = block
        halo_copies(group)[0].start()
        for i in range(HALO):
            re, im = result[2 * i], result[2 * i + 1]
            row = 8 * (group * HALO + i)
            ylo[row : row + 8, :] = jnp.where(low4, re[:8], pltpu.roll(im[:8], 4, axis=0))
            yhi[row : row + 8, :] = jnp.where(low4, pltpu.roll(re[8:], 4, axis=0), im[8:])
        for copy in halo_copies(group)[1:]:
            copy.start()

    lax.fori_loop(0, OWN // 32, split_rows, 0)
    grid[...] = triple(wbuf[0, :, :OWN], wbuf[1, :, :OWN], exth[:OWN], extl[:OWN])
    for group in range(2):
        for copy in halo_copies(group):
            copy.wait_recv()
    lax.fori_loop(OWN // 32, EXT // 32, split_rows, 0)

    def shard_copy(group, step):
        peer = ring(step)
        return pltpu.make_async_remote_copy(
            src_ref=fin.at[group, pl.ds(pl.multiple_of(peer * TL, TL), TL), :],
            dst_ref=obuf.at[group, me],
            send_sem=bsend.at[group, step],
            recv_sem=brecv.at[group, step],
            device_id=(peer, gx),
            device_id_type=MESH,
        )

    mine = [
        pltpu.make_async_copy(
            fin.at[group, pl.ds(pl.multiple_of(me * TL, TL), TL), :], obuf.at[group, me], local_sem.at[group]
        )
        for group in range(2)
    ]
    for group in range(2):
        rows = slice(group * OWN // 2, (group + 1) * OWN // 2)
        grid[rows, :] += triple(wbuf[0, rows, OWN:], wbuf[1, rows, OWN:], exth[OWN:], extl[OWN:])
        kick(group)
        fin[group] = jnp.concatenate(disperse(group), axis=0).T
        for step in order:
            shard_copy(group, step).start()
        mine[group].start()

    for q in range(TL // TC):
        for copy in row_copies(q):
            copy.wait_send()
    for group, index, first, count in messages:
        for step in order:
            column_copy(group, index, step, first, count).wait_send()
    for group in range(2):
        for copy in halo_copies(group):
            copy.wait_send()

    slot = lax.broadcasted_iota(jnp.int32, (TL, 128), 1) // YC
    for group in range(2):
        mine[group].wait()
        for step in order:
            shard_copy(group, step).wait_recv()
        for h in range(2):
            turned = []
            for jj in range(8):
                part = obuf[group, h * 8 + jj]
                turned.append(pltpu.roll(part, YC * jj, axis=1) if jj else part)
            for s in range(8):
                piece = turned[0]
                for jj in range(1, 8):
                    piece = jnp.where(slot == (jj + s) % 8, turned[jj], piece)
                if s:
                    piece = pltpu.roll(piece, 128 - YC * s, axis=1)
                stage[h, pl.ds((s % 2) * TL * XR + group * HALO + s // 2, TL, stride=XR), :] = piece
    for h in range(2):
        out[:, h * 128 : (h + 1) * 128] = stage[h]
    for group in range(2):
        for step in order:
            shard_copy(group, step).wait_send()


def per_device(envelope, density_map, disp_phase):
    rows = 2 * TL * XR
    vmem = pl.BlockSpec(memory_space=pltpu.VMEM)
    anywhere = pl.BlockSpec(memory_space=pltpu.HBM)
    dma = pltpu.SemaphoreType.DMA
    result = pl.pallas_call(
        kernel,
        out_shape=jax.ShapeDtypeStruct((rows, NY), F32),
        in_specs=[anywhere, vmem, vmem, anywhere, anywhere],
        out_specs=vmem,
        scratch_shapes=[
            pltpu.VMEM((2, rows, 128), F32),
            pltpu.VMEM((XR + 2 * HALO, 2, TL, NY), F32),
            pltpu.VMEM((2, NZ, TL, 128), F32),
            pltpu.VMEM((2, NT, 128), F32),
            pltpu.VMEM((EXT, NT), F32),
            pltpu.VMEM((EXT, NT), BF16),
            pltpu.VMEM((EXT, NT), BF16),
            pltpu.VMEM((8 * XR, NT), F32),
            pltpu.VMEM((8 * XR, NT), F32),
            pltpu.VMEM((NT, 2 * NT), BF16),
            pltpu.VMEM((NT, 2 * NT), BF16),
            pltpu.VMEM((NT, NT), BF16),
            pltpu.VMEM((2, OWN, EXT), BF16),
            pltpu.VMEM((2, NT, NT), F32),
            pltpu.VMEM((CELLS, NT), F32),
            pltpu.VMEM((OWN, NT), F32),
            pltpu.VMEM((CELLS, NT), F32),
            pltpu.VMEM((CELLS, NT), BF16),
            pltpu.VMEM((CELLS, NT), BF16),
            pltpu.VMEM((CELLS, NT), F32),
            pltpu.VMEM((OWN, NT), BF16),
            pltpu.VMEM((OWN, NT), BF16),
            pltpu.VMEM((OWN, 2 * NT), F32),
            pltpu.VMEM((2, NT, 128), F32),
            pltpu.VMEM((2, NZ, TL, 128), F32),
            dma((6,)),
            dma((TL // TC, 2)),
            dma((TL // TC, 2)),
            dma((3, NZ)),
            dma((3, NZ)),
            dma((10,)),
            dma((10,)),
            dma((2, NZ)),
            dma((2, NZ)),
        ],
        compiler_params=pltpu.CompilerParams(
            collective_id=0, has_side_effects=True, vmem_limit_bytes=53 * 1024 * 1024
        ),
        name="filament",
    )(
        envelope.reshape(rows, NY),
        density_map,
        disp_phase.reshape(1, NT),
        jnp.asarray(diffraction_matrices()),
        jnp.asarray(fourier_matrices()),
    )
    return result.reshape(2, TL, XR, NY)


def solution(mesh):
    placed = (P(None, "ta", "gx", None), P("gx", None), P())
    return jax.shard_map(
        per_device, mesh=mesh, in_specs=placed, out_specs=P(None, "ta", "gx", None), check_vma=False
    )
```

```python
import functools
import math

import jax
import jax.numpy as jnp
import ml_dtypes
import numpy as np
from jax import lax
from jax.experimental import pallas as pl
from jax.experimental.pallas import tpu as pltpu
from jax.sharding import PartitionSpec as P

MESH = pl.DeviceIdType.MESH
F32 = jnp.float32
BF16 = jnp.bfloat16

STEPS = 2
NT = 512
NZ = 16
TL = NT // NZ
NG = 32
XR = 8
NY = 256
YC = NY // NZ
CELLS = XR * YC
OWN = 2 * CELLS
HALO = 4
TC = 8
PAIR = 2 * YC

LEFT = OWN
RIGHT = LEFT + 8 * XR
DOWN = RIGHT + 8 * XR
UP = DOWN + HALO * PAIR + 48
EXT = UP + HALO * PAIR + 48

diffract_step = 0.25
ionize_gain = 0.4
kerr_gain = 0.5
plasma_gain = 1.0
absorb_gain = 0.05


def row_cells():
    rows = []
    for x in range(XR):
        for c in range(2):
            for y in range(YC):
                rows.append((x, y, c))
    for base in (-HALO, YC):
        for x in range(XR):
            for c in range(2):
                for y in range(HALO):
                    rows.append((x, base + y, c))
    for xbase in (XR, -HALO):
        for x in range(HALO):
            for c in range(2):
                for y in range(YC):
                    rows.append((xbase + x, y, c))
        for ybase in (-HALO, YC):
            for x in range(3):
                for c in range(2):
                    for y in range(HALO):
                        rows.append((max(xbase, -3) + x, ybase + y, c))
    return rows


def diffraction_matrices():
    rows = row_cells()
    wide, high = YC + 2 * HALO, XR + 2 * HALO
    result = np.zeros((9, 2, OWN, EXT), ml_dtypes.bfloat16)
    for vx in range(3):
        for vy in range(3):
            inside = np.ones((high, wide), bool)
            if vx == 0:
                inside[:HALO] = False
            if vx == 2:
                inside[-HALO:] = False
            if vy == 0:
                inside[:, :HALO] = False
            if vy == 2:
                inside[:, -HALO:] = False
            count = high * wide
            lap = np.zeros((count, count))
            for x in range(high):
                for y in range(wide):
                    if not inside[x, y]:
                        continue
                    lap[x * wide + y, x * wide + y] = -4.0
                    for dx, dy in ((1, 0), (-1, 0), (0, 1), (0, -1)):
                        a, b = x + dx, y + dy
                        if 0 <= a < high and 0 <= b < wide and inside[a, b]:
                            lap[x * wide + y, a * wide + b] = 1.0
            own = [(x + HALO) * wide + y + HALO for x in range(XR) for y in range(YC)]
            power = np.eye(count)[own].astype(complex)
            total = power.copy()
            for n in range(1, 5):
                power = power @ lap * (1j * diffract_step / n)
                total = total + power
            place = {(x, y): i for i, (x, y) in enumerate((x, y) for x in range(XR) for y in range(YC))}
            matrix = np.zeros((OWN, EXT))
            for out_row, (x, y, c) in enumerate(rows[:OWN]):
                line = total[place[(x, y)]]
                for col, (a, b, d) in enumerate(rows):
                    value = line[(a + HALO) * wide + b + HALO]
                    if c == d:
                        matrix[out_row, col] = value.real
                    else:
                        matrix[out_row, col] = -value.imag if c == 0 else value.imag
            matrix = matrix.astype(np.float32)
            upper = matrix.astype(ml_dtypes.bfloat16)
            result[vx * 3 + vy, 0] = upper
            result[vx * 3 + vy, 1] = (matrix - upper.astype(np.float32)).astype(ml_dtypes.bfloat16)
    return result


def fourier_matrices():
    index = np.arange(NT)
    angles = (index[:, None] * index[None, :] % NT) * (2.0 * math.pi / NT)
    return np.stack([np.cos(angles), np.sin(angles)]).astype(np.float32)


def split(value):
    upper = value.astype(BF16)
    return upper, (value - upper.astype(F32)).astype(BF16)


def dot(a, b):
    return jnp.dot(a, b, preferred_element_type=F32)


def triple(ah, al, bh, bl):
    return dot(ah, bh) + dot(ah, bl) + dot(al, bh)


def sincos(angle):
    turns = jnp.floor(angle * (2.0 / math.pi) + 0.5)
    rest = ((angle - turns * 1.5703125) - turns * 4.837512969970703125e-4) - turns * 7.54978995489188216e-8
    quarter = turns.astype(jnp.int32)
    z = rest * rest
    sine = ((-1.9515295891e-4 * z + 8.3321608736e-3) * z - 1.6666654611e-1) * (z * rest) + rest
    cosine = ((2.443315711809948e-5 * z - 1.388731625493765e-3) * z + 4.166664568298827e-2) * (z * z) + (1.0 - 0.5 * z)
    odd = (quarter & 1) == 1
    a = jnp.where(odd, cosine, sine)
    b = jnp.where(odd, sine, cosine)
    a = jnp.where((quarter & 2) == 2, -a, a)
    b = jnp.where(((quarter + 1) & 2) == 2, -b, b)
    return a, b


def lap_powers(halves, above, below, first, last):
    result = []
    for number in range(1, HALO + 1):
        centre = [part[TC:-TC] for part in halves]
        rows = centre[0].shape[0]
        up = [pltpu.roll(part, 1, axis=1) for part in centre]
        down = [pltpu.roll(part, 127, axis=1) for part in centre]
        beside = [
            jnp.where(first[:rows], 0.0, up[0]) + jnp.where(last[:rows], down[1], down[0]),
            jnp.where(first[:rows], up[0], up[1]) + jnp.where(last[:rows], 0.0, down[1]),
        ]
        rest = (HALO - number) * TC
        out = []
        for part, mid, across in zip(halves, centre, beside):
            lapped = (part[2 * TC :] + part[: -2 * TC]) + (across - 4.0 * mid)
            if rest:
                lapped = jnp.concatenate([lapped[:rest] * above, lapped[rest:-rest], lapped[-rest:] * below], axis=0)
            out.append(lapped)
        halves = out
        result.append([part[rest:-rest] if rest else part for part in halves])
    return result


def diffract(re, im, above, below, first, last):
    edge = HALO * TC
    by_re = lap_powers(re, above, below, first, last)
    by_im = lap_powers(im, above, below, first, last)
    a1, a2, a3, a4 = (diffract_step**n / math.factorial(n) for n in range(1, 5))
    out = []
    for h in range(2):
        r1, r2, r3, r4 = (by_re[n][h] for n in range(4))
        i1, i2, i3, i4 = (by_im[n][h] for n in range(4))
        out.append(
            (
                re[h][edge:-edge] - a1 * i1 - a2 * r2 + a3 * i3 + a4 * r4,
                im[h][edge:-edge] + a1 * r1 - a2 * i2 - a3 * r3 + a4 * i4,
            )
        )
    return out


def kernel(
    env, dens_hbm, phase_hbm, wmat, fourier, out,
    dens, phase, stage, field, sbuf, rbuf, ext, exth, extl, ylo, yhi, ch, cl, tri, wbuf, fbuf, dcol,
    grid, inten, rh, rl, plasma, uh, ul, spec, fin, obuf,
    heard, local_sem, xsend, xrecv, asend, arecv, hsend, hrecv, bsend, brecv,
):
    me = lax.axis_index("ta")
    gx = lax.axis_index("gx")

    loads = [
        pltpu.make_async_copy(env.at[:, pl.ds(h * 128, 128)], stage.at[h], local_sem.at[4 + h]) for h in range(2)
    ]
    for load in loads:
        load.start()
    variant = (lax.div(gx + NG - 2, NG - 1) + lax.div(gx, NG - 1)) * 3 + lax.div(me + NZ - 2, NZ - 1) + lax.div(me, NZ - 1)
    load_w = pltpu.make_async_copy(wmat.at[variant], wbuf, local_sem.at[2])
    load_w.start()
    load_f = pltpu.make_async_copy(fourier, fbuf, local_sem.at[3])
    load_f.start()
    small = [
        pltpu.make_async_copy(dens_hbm, dens, local_sem.at[6]),
        pltpu.make_async_copy(phase_hbm, phase, local_sem.at[7]),
    ]
    for load in small:
        load.start()

    def ring(step):
        return lax.rem(me + step + NZ, NZ)

    def side(step):
        return lax.rem(gx + step + NG, NG)

    barrier = pltpu.get_barrier_semaphore()
    for dx in (0, -1, 1):
        for dz in (-1, 0, 1):
            if dx or dz:
                pl.semaphore_signal(barrier, inc=1, device_id=(ring(dz), side(dx)), device_id_type=MESH)

    def tell(level):
        for way in (-1, 1):
            pl.semaphore_signal(
                heard.at[level], inc=1, device_id=(ring(way * (1 << level)), gx), device_id_type=MESH
            )

    def hear(level):
        pl.semaphore_wait(heard.at[level], 2)

    for load in loads:
        load.wait()
    for h in range(2):
        for c in range(2):
            for x in range(XR):
                field[HALO + x, c, :, h * 128 : (h + 1) * 128] = stage[h, pl.ds(c * TL * XR + x, TL, stride=XR), :]

    pl.semaphore_wait(barrier, 8)
    tell(0)

    def row_copies(q):
        times = pl.ds(pl.multiple_of(q * TC, TC), TC)
        return [
            pltpu.make_async_remote_copy(
                src_ref=field.at[pl.ds(source, HALO), :, times, :],
                dst_ref=field.at[pl.ds(target, HALO), :, times, :],
                send_sem=xsend.at[q, way],
                recv_sem=xrecv.at[q, way],
                device_id=(me, side(dx)),
                device_id_type=MESH,
            )
            for way, (source, target, dx) in enumerate(((XR, 0, 1), (HALO, HALO + XR, -1)))
        ]

    for q in range(TL // TC):
        for copy in row_copies(q):
            copy.start()
    hear(0)
    tell(1)
    hear(1)
    tell(2)

    def column_copy(group, index, step, first, count):
        peer = ring(step)
        return pltpu.make_async_remote_copy(
            src_ref=sbuf.at[group, peer, pl.ds(first, count), :],
            dst_ref=rbuf.at[group, pl.ds(pl.multiple_of(me * TL, TL) + first, count), :],
            send_sem=asend.at[index, step],
            recv_sem=arecv.at[index, step],
            device_id=(peer, gx),
            device_id_type=MESH,
        )

    order = [s for k in range(8, 0, -1) for s in ((k, NZ - k) if k < 8 else (8,))]
    messages = ((0, 0, 0, TL // 2), (0, 1, TL // 2, TL // 2), (1, 2, 0, TL))
    above = jnp.where(gx == 0, 0.0, 1.0).astype(F32)
    below = jnp.where(gx == NG - 1, 0.0, 1.0).astype(F32)

    def first_diffraction(q, carry):
        times = pl.ds(pl.multiple_of(q * TC, TC), TC)
        for copy in row_copies(q):
            copy.wait_recv()
        lane = lax.broadcasted_iota(jnp.int32, ((XR + 2 * HALO) * TC, 128), 1)
        slot = lax.broadcasted_iota(jnp.int32, (TC, 128), 1) // YC
        parts = []
        for c in range(2):
            halves = []
            for h in range(2):
                value = field[:, c, times, h * 128 : (h + 1) * 128]
                value = jnp.concatenate([value[:HALO] * above, value[HALO:-HALO], value[-HALO:] * below], axis=0)
                halves.append(value.reshape((XR + 2 * HALO) * TC, 128))
            parts.append(halves)
        parts = diffract(parts[0], parts[1], above, below, lane == 0, lane == 127)
        for h in range(2):
            for group in range(2):
                turned = []
                for s in range(8):
                    first = (group * HALO + s // 2) * TC
                    part = parts[h][s % 2][first : first + TC]
                    turned.append(pltpu.roll(part, YC * s, axis=1) if s else part)
                for jj in range(8):
                    piece = turned[0]
                    for s in range(1, 8):
                        piece = jnp.where(slot == (jj + s) % 8, turned[s], piece)
                    if jj:
                        piece = pltpu.roll(piece, 128 - YC * jj, axis=1)
                    sbuf[group, h * 8 + jj, times, :] = piece
        return carry

    half = TL // TC // 2
    lax.fori_loop(0, half, first_diffraction, 0)
    hear(2)
    for step in order:
        column_copy(*messages[0][:2], step, *messages[0][2:]).start()
    lax.fori_loop(half, 2 * half, first_diffraction, 0)
    for group, index, first, count in messages[1:]:
        for step in order:
            column_copy(group, index, step, first, count).start()
    mine = [
        pltpu.make_async_copy(
            sbuf.at[group, me], rbuf.at[group, pl.ds(pl.multiple_of(me * TL, TL), TL), :], local_sem.at[group]
        )
        for group in range(2)
    ]
    for copy in mine:
        copy.start()

    load_f.wait()
    for load in small:
        load.wait()
    turn = phase[...]
    sine, cosine = sincos(turn)
    pair = jnp.concatenate([cosine, sine] * 4, axis=0) * (1.0 / NT)
    by_cos = jnp.dot(pair, fbuf[0], precision=lax.Precision.HIGHEST, preferred_element_type=F32)
    by_sin = jnp.dot(pair, fbuf[1], precision=lax.Precision.HIGHEST, preferred_element_type=F32)
    rows16 = lax.broadcasted_iota(jnp.int32, (16, NT), 0)
    for part, line in enumerate((by_cos[0:1] - by_sin[1:2], by_sin[0:1] + by_cos[1:2])):
        base = jnp.broadcast_to(line, (16, NT))
        for bit in range(4):
            base = jnp.where((rows16 >> bit) & 1 == 1, pltpu.roll(base, 1 << bit, axis=1), base)
        for block in range(NT // 16):
            high, low = split(pltpu.roll(base, 16 * block, axis=1) if block else base)
            ch[16 * block : 16 * block + 16, part * NT : (part + 1) * NT] = high
            cl[16 * block : 16 * block + 16, part * NT : (part + 1) * NT] = low

    def tri_rows(block, carry):
        first = pl.multiple_of(block * 16, 16)
        row = lax.broadcasted_iota(jnp.int32, (16, NT), 0) + first
        col = lax.broadcasted_iota(jnp.int32, (16, NT), 1)
        tri[pl.ds(first, 16), :] = jnp.where(row < col, 1.0, 0.0).astype(BF16)
        return carry

    lax.fori_loop(0, NT // 16, tri_rows, 0)
    lane = lax.broadcasted_iota(jnp.int32, (YC, NY), 1)
    row = lax.broadcasted_iota(jnp.int32, (YC, NY), 0)
    wanted = lane == row + me * YC
    for x in range(XR):
        line = jnp.broadcast_to(dens[x : x + 1, :], (YC, NY))
        column = jnp.sum(jnp.where(wanted, line, 0.0), axis=1, keepdims=True)
        dcol[x * YC : (x + 1) * YC, :] = jnp.broadcast_to(column * (ionize_gain / NT), (YC, NT))
    load_w.wait()

    def kick(group):
        def rates(x, carry):
            first = pl.multiple_of(x * PAIR, PAIR)
            place = pl.ds(pl.multiple_of(x * YC, YC), YC)
            re = grid[pl.ds(first, YC), :]
            im = grid[pl.ds(first + YC, YC), :]
            intensity = re * re + im * im
            inten[place, :] = intensity
            high, low = split(dcol[place, :] * intensity * intensity)
            rh[place, :] = high
            rl[place, :] = low
            return carry

        lax.fori_loop(group * HALO, (group + 1) * HALO, rates, 0, unroll=True)
        cells = slice(group * CELLS // 2, (group + 1) * CELLS // 2)
        plasma[cells, :] = dot(rh[cells, :], tri[...]) + dot(rl[cells, :], tri[...])

        def turn(x, carry):
            first = pl.multiple_of(x * PAIR, PAIR)
            place = pl.ds(pl.multiple_of(x * YC, YC), YC)
            re = grid[pl.ds(first, YC), :]
            im = grid[pl.ds(first + YC, YC), :]
            earlier = plasma[place, :]
            sine, cosine = sincos(kerr_gain * inten[place, :] - plasma_gain * earlier)
            amplitude = jnp.exp(-absorb_gain * earlier)
            sine = sine * amplitude
            cosine = cosine * amplitude
            high, low = split(re * cosine - im * sine)
            uh[pl.ds(first, YC), :] = high
            ul[pl.ds(first, YC), :] = low
            high, low = split(re * sine + im * cosine)
            uh[pl.ds(first + YC, YC), :] = high
            ul[pl.ds(first + YC, YC), :] = low
            return carry

        lax.fori_loop(group * HALO, (group + 1) * HALO, turn, 0, unroll=True)

    def disperse(group):
        rows = slice(group * OWN // 2, (group + 1) * OWN // 2)
        both = dot(jnp.concatenate([uh[rows, :], ul[rows, :]], axis=0), ch[...])
        spec[rows, :] = both[: OWN // 2] + both[OWN // 2 :] + dot(uh[rows, :], cl[...])
        result = []
        for x in range(group * HALO, (group + 1) * HALO):
            re = spec[x * PAIR : x * PAIR + YC, :]
            im = spec[x * PAIR + YC : (x + 1) * PAIR, :]
            result.append(re[:, :NT] - im[:, NT:])
            result.append(re[:, NT:] + im[:, :NT])
        return result

    def halo_copy(index, source, first, dx, dz):
        return pltpu.make_async_remote_copy(
            src_ref=source,
            dst_ref=ext.at[pl.ds(first, source.shape[0]), :],
            send_sem=hsend.at[index],
            recv_sem=hrecv.at[index],
            device_id=(ring(dz), side(dx)),
            device_id_type=MESH,
        )

    def halo_copies(group):
        rows = pl.ds(group * 32, 32)
        towards = 2 * group - 1
        end = pl.ds(40 * group, 24)
        return [
            halo_copy(5 * group, ext.at[pl.ds(group * OWN // 2, OWN // 2), :], UP if group else DOWN, towards, 0),
            halo_copy(5 * group + 1, yhi.at[rows, :], LEFT + 32 * group, 0, 1),
            halo_copy(5 * group + 2, ylo.at[rows, :], RIGHT + 32 * group, 0, -1),
            halo_copy(5 * group + 3, yhi.at[end, :], (UP if group else DOWN) + HALO * PAIR, towards, 1),
            halo_copy(5 * group + 4, ylo.at[end, :], (UP if group else DOWN) + HALO * PAIR + 24, towards, -1),
        ]

    def split_rows(block, carry):
        place = pl.ds(pl.multiple_of(block * 16, 16), 16)
        high, low = split(ext[place, :])
        exth[place, :] = high
        extl[place, :] = low
        return carry

    low4 = lax.broadcasted_iota(jnp.int32, (8, NT), 0) < HALO
    for group in range(2):
        mine[group].wait()
        for g, index, first, count in messages:
            if g == group:
                for step in order:
                    column_copy(g, index, step, first, count).wait_recv()
        base = group * OWN // 2
        grid[base : base + OWN // 2, :] = rbuf[group].T
        kick(group)
        result = disperse(group)
        for i, block in enumerate(result):
            ext[base + i * YC : base + (i + 1) * YC, :] = block
        halo_copies(group)[0].start()
        for i in range(HALO):
            re, im = result[2 * i], result[2 * i + 1]
            row = 8 * (group * HALO + i)
            ylo[row : row + 8, :] = jnp.where(low4, re[:8], pltpu.roll(im[:8], 4, axis=0))
            yhi[row : row + 8, :] = jnp.where(low4, pltpu.roll(re[8:], 4, axis=0), im[8:])
        for copy in halo_copies(group)[1:]:
            copy.start()

    lax.fori_loop(0, OWN // 16, split_rows, 0)
    both = dot(jnp.concatenate([wbuf[0, :, :OWN], wbuf[1, :, :OWN]], axis=0), exth[:OWN])
    grid[...] = both[:OWN] + both[OWN:] + dot(wbuf[0, :, :OWN], extl[:OWN])

    def shard_copy(group, step):
        peer = ring(step)
        return pltpu.make_async_remote_copy(
            src_ref=fin.at[group, pl.ds(pl.multiple_of(peer * TL, TL), TL), :],
            dst_ref=obuf.at[group, me],
            send_sem=bsend.at[group, step],
            recv_sem=brecv.at[group, step],
            device_id=(peer, gx),
            device_id_type=MESH,
        )

    mine = [
        pltpu.make_async_copy(
            fin.at[group, pl.ds(pl.multiple_of(me * TL, TL), TL), :], obuf.at[group, me], local_sem.at[group]
        )
        for group in range(2)
    ]
    for group in (1, 0):
        for index in (1, 2) if group else ():
            for g in range(2):
                halo_copies(g)[index].wait_recv()
        for index in (0, 3, 4):
            halo_copies(1 - group)[index].wait_recv()
        rows = slice(group * OWN // 2, (group + 1) * OWN // 2)
        first = OWN if group else UP
        lax.fori_loop(first // 16, (first + (UP - OWN if group else EXT - UP)) // 16, split_rows, 0)
        if group:
            grid[rows, :] += triple(wbuf[0, rows, OWN:UP], wbuf[1, rows, OWN:UP], exth[OWN:UP], extl[OWN:UP])
        else:
            for a, b in ((OWN, DOWN), (UP, EXT)):
                grid[rows, :] += triple(wbuf[0, rows, a:b], wbuf[1, rows, a:b], exth[a:b], extl[a:b])
        kick(group)
        fin[group] = jnp.concatenate(disperse(group), axis=0).T
        for step in order:
            shard_copy(group, step).start()
        mine[group].start()

    for q in range(TL // TC):
        for copy in row_copies(q):
            copy.wait_send()
    for group, index, first, count in messages:
        for step in order:
            column_copy(group, index, step, first, count).wait_send()
    for group in range(2):
        for copy in halo_copies(group):
            copy.wait_send()

    slot = lax.broadcasted_iota(jnp.int32, (TL, 128), 1) // YC
    for group in (1, 0):
        mine[group].wait()
        for step in order:
            shard_copy(group, step).wait_recv()
        for h in range(2):
            turned = []
            for jj in range(8):
                part = obuf[group, h * 8 + jj]
                turned.append(pltpu.roll(part, YC * jj, axis=1) if jj else part)
            for s in range(8):
                piece = turned[0]
                for jj in range(1, 8):
                    piece = jnp.where(slot == (jj + s) % 8, turned[jj], piece)
                if s:
                    piece = pltpu.roll(piece, 128 - YC * s, axis=1)
                stage[h, pl.ds((s % 2) * TL * XR + group * HALO + s // 2, TL, stride=XR), :] = piece
    for h in range(2):
        out[:, h * 128 : (h + 1) * 128] = stage[h]
    for group in range(2):
        for step in order:
            shard_copy(group, step).wait_send()


def per_device(envelope, density_map, disp_phase):
    rows = 2 * TL * XR
    vmem = pl.BlockSpec(memory_space=pltpu.VMEM)
    anywhere = pl.BlockSpec(memory_space=pltpu.HBM)
    dma = pltpu.SemaphoreType.DMA
    result = pl.pallas_call(
        kernel,
        out_shape=jax.ShapeDtypeStruct((rows, NY), F32),
        in_specs=[anywhere] * 5,
        out_specs=vmem,
        scratch_shapes=[
            pltpu.VMEM((XR, NY), F32),
            pltpu.VMEM((1, NT), F32),
            pltpu.VMEM((2, rows, 128), F32),
            pltpu.VMEM((XR + 2 * HALO, 2, TL, NY), F32),
            pltpu.VMEM((2, NZ, TL, 128), F32),
            pltpu.VMEM((2, NT, 128), F32),
            pltpu.VMEM((EXT, NT), F32),
            pltpu.VMEM((EXT, NT), BF16),
            pltpu.VMEM((EXT, NT), BF16),
            pltpu.VMEM((8 * XR, NT), F32),
            pltpu.VMEM((8 * XR, NT), F32),
            pltpu.VMEM((NT, 2 * NT), BF16),
            pltpu.VMEM((NT, 2 * NT), BF16),
            pltpu.VMEM((NT, NT), BF16),
            pltpu.VMEM((2, OWN, EXT), BF16),
            pltpu.VMEM((2, NT, NT), F32),
            pltpu.VMEM((CELLS, NT), F32),
            pltpu.VMEM((OWN, NT), F32),
            pltpu.VMEM((CELLS, NT), F32),
            pltpu.VMEM((CELLS, NT), BF16),
            pltpu.VMEM((CELLS, NT), BF16),
            pltpu.VMEM((CELLS, NT), F32),
            pltpu.VMEM((OWN, NT), BF16),
            pltpu.VMEM((OWN, NT), BF16),
            pltpu.VMEM((OWN, 2 * NT), F32),
            pltpu.VMEM((2, NT, 128), F32),
            pltpu.VMEM((2, NZ, TL, 128), F32),
            pltpu.SemaphoreType.REGULAR((3,)),
            dma((8,)),
            dma((TL // TC, 2)),
            dma((TL // TC, 2)),
            dma((3, NZ)),
            dma((3, NZ)),
            dma((10,)),
            dma((10,)),
            dma((2, NZ)),
            dma((2, NZ)),
        ],
        compiler_params=pltpu.CompilerParams(
            collective_id=0, has_side_effects=True, vmem_limit_bytes=53 * 1024 * 1024
        ),
        name="filament",
    )(
        envelope.reshape(rows, NY),
        density_map,
        disp_phase.reshape(1, NT),
        jnp.asarray(diffraction_matrices()),
        jnp.asarray(fourier_matrices()),
    )
    return result.reshape(2, TL, XR, NY)


def solution(mesh):
    placed = (P(None, "ta", "gx", None), P("gx", None), P())
    return jax.shard_map(
        per_device, mesh=mesh, in_specs=placed, out_specs=P(None, "ta", "gx", None), check_vma=False
    )
```

```python
import functools
import math

import jax
import jax.numpy as jnp
import ml_dtypes
import numpy as np
from jax import lax
from jax.experimental import pallas as pl
from jax.experimental.pallas import tpu as pltpu
from jax.sharding import PartitionSpec as P

MESH = pl.DeviceIdType.MESH
F32 = jnp.float32
BF16 = jnp.bfloat16

STEPS = 2
NT = 512
NZ = 16
TL = NT // NZ
NG = 32
XR = 8
NY = 256
YC = NY // NZ
CELLS = XR * YC
OWN = 2 * CELLS
HALO = 4
TC = 8
PAIR = 2 * YC

LEFT = OWN
RIGHT = LEFT + 8 * XR
DOWN = RIGHT + 8 * XR
UP = DOWN + HALO * PAIR + 48
EXT = UP + HALO * PAIR + 48

diffract_step = 0.25
ionize_gain = 0.4
kerr_gain = 0.5
plasma_gain = 1.0
absorb_gain = 0.05


def row_cells():
    rows = []
    for x in range(XR):
        for c in range(2):
            for y in range(YC):
                rows.append((x, y, c))
    for base in (-HALO, YC):
        for x in range(XR):
            for c in range(2):
                for y in range(HALO):
                    rows.append((x, base + y, c))
    for xbase in (XR, -HALO):
        for x in range(HALO):
            for c in range(2):
                for y in range(YC):
                    rows.append((xbase + x, y, c))
        for ybase in (-HALO, YC):
            for x in range(3):
                for c in range(2):
                    for y in range(HALO):
                        rows.append((max(xbase, -3) + x, ybase + y, c))
    return rows


def diffraction_matrices():
    rows = row_cells()
    wide, high = YC + 2 * HALO, XR + 2 * HALO
    result = np.zeros((9, 2, OWN, EXT), ml_dtypes.bfloat16)
    for vx in range(3):
        for vy in range(3):
            inside = np.ones((high, wide), bool)
            if vx == 0:
                inside[:HALO] = False
            if vx == 2:
                inside[-HALO:] = False
            if vy == 0:
                inside[:, :HALO] = False
            if vy == 2:
                inside[:, -HALO:] = False
            count = high * wide
            lap = np.zeros((count, count))
            for x in range(high):
                for y in range(wide):
                    if not inside[x, y]:
                        continue
                    lap[x * wide + y, x * wide + y] = -4.0
                    for dx, dy in ((1, 0), (-1, 0), (0, 1), (0, -1)):
                        a, b = x + dx, y + dy
                        if 0 <= a < high and 0 <= b < wide and inside[a, b]:
                            lap[x * wide + y, a * wide + b] = 1.0
            own = [(x + HALO) * wide + y + HALO for x in range(XR) for y in range(YC)]
            power = np.eye(count)[own].astype(complex)
            total = power.copy()
            for n in range(1, 5):
                power = power @ lap * (1j * diffract_step / n)
                total = total + power
            place = {(x, y): i for i, (x, y) in enumerate((x, y) for x in range(XR) for y in range(YC))}
            matrix = np.zeros((OWN, EXT))
            for out_row, (x, y, c) in enumerate(rows[:OWN]):
                line = total[place[(x, y)]]
                for col, (a, b, d) in enumerate(rows):
                    value = line[(a + HALO) * wide + b + HALO]
                    if c == d:
                        matrix[out_row, col] = value.real
                    else:
                        matrix[out_row, col] = -value.imag if c == 0 else value.imag
            matrix = matrix.astype(np.float32)
            upper = matrix.astype(ml_dtypes.bfloat16)
            result[vx * 3 + vy, 0] = upper
            result[vx * 3 + vy, 1] = (matrix - upper.astype(np.float32)).astype(ml_dtypes.bfloat16)
    return result


def fourier_matrices():
    index = np.arange(NT)
    angles = (index[:, None] * index[None, :] % NT) * (2.0 * math.pi / NT)
    return np.stack([np.cos(angles), np.sin(angles)]).astype(np.float32)


def split(value):
    upper = value.astype(BF16)
    return upper, (value - upper.astype(F32)).astype(BF16)


def dot(a, b):
    return jnp.dot(a, b, preferred_element_type=F32)


def triple(ah, al, bh, bl):
    return dot(ah, bh) + dot(ah, bl) + dot(al, bh)


def sincos(angle):
    turns = jnp.floor(angle * (2.0 / math.pi) + 0.5)
    rest = ((angle - turns * 1.5703125) - turns * 4.837512969970703125e-4) - turns * 7.54978995489188216e-8
    quarter = turns.astype(jnp.int32)
    z = rest * rest
    sine = ((-1.9515295891e-4 * z + 8.3321608736e-3) * z - 1.6666654611e-1) * (z * rest) + rest
    cosine = ((2.443315711809948e-5 * z - 1.388731625493765e-3) * z + 4.166664568298827e-2) * (z * z) + (1.0 - 0.5 * z)
    odd = (quarter & 1) == 1
    a = jnp.where(odd, cosine, sine)
    b = jnp.where(odd, sine, cosine)
    a = jnp.where((quarter & 2) == 2, -a, a)
    b = jnp.where(((quarter + 1) & 2) == 2, -b, b)
    return a, b


def lap_powers(halves, above, below, first, last):
    result = []
    for number in range(1, HALO + 1):
        centre = [part[TC:-TC] for part in halves]
        rows = centre[0].shape[0]
        up = [pltpu.roll(part, 1, axis=1) for part in centre]
        down = [pltpu.roll(part, 127, axis=1) for part in centre]
        beside = [
            jnp.where(first[:rows], 0.0, up[0]) + jnp.where(last[:rows], down[1], down[0]),
            jnp.where(first[:rows], up[0], up[1]) + jnp.where(last[:rows], 0.0, down[1]),
        ]
        rest = (HALO - number) * TC
        out = []
        for part, mid, across in zip(halves, centre, beside):
            lapped = (part[2 * TC :] + part[: -2 * TC]) + (across - 4.0 * mid)
            if rest:
                lapped = jnp.concatenate([lapped[:rest] * above, lapped[rest:-rest], lapped[-rest:] * below], axis=0)
            out.append(lapped)
        halves = out
        result.append([part[rest:-rest] if rest else part for part in halves])
    return result


def diffract(re, im, above, below, first, last):
    edge = HALO * TC
    by_re = lap_powers(re, above, below, first, last)
    by_im = lap_powers(im, above, below, first, last)
    a1, a2, a3, a4 = (diffract_step**n / math.factorial(n) for n in range(1, 5))
    out = []
    for h in range(2):
        r1, r2, r3, r4 = (by_re[n][h] for n in range(4))
        i1, i2, i3, i4 = (by_im[n][h] for n in range(4))
        out.append(
            (
                re[h][edge:-edge] - a1 * i1 - a2 * r2 + a3 * i3 + a4 * r4,
                im[h][edge:-edge] + a1 * r1 - a2 * i2 - a3 * r3 + a4 * i4,
            )
        )
    return out


def kernel(
    env, small, wmat, fourier, out,
    dens, stage, field, sbuf, rbuf, ext, exth, extl, ylo, yhi, ch, cl, tri, wbuf, fbuf, dcol,
    grid, inten, rh, rl, plasma, uh, ul, fin, obuf,
    heard, local_sem, xsend, xrecv, asend, arecv, hsend, hrecv, bsend, brecv,
):
    me = lax.axis_index("ta")
    gx = lax.axis_index("gx")

    loads = [
        pltpu.make_async_copy(env.at[:, pl.ds(h * 128, 128)], stage.at[h], local_sem.at[4 + h]) for h in range(2)
    ]
    for load in loads:
        load.start()
    variant = (lax.div(gx + NG - 2, NG - 1) + lax.div(gx, NG - 1)) * 3 + lax.div(me + NZ - 2, NZ - 1) + lax.div(me, NZ - 1)
    load_w = pltpu.make_async_copy(wmat.at[variant], wbuf, local_sem.at[2])
    load_w.start()
    load_f = pltpu.make_async_copy(fourier, fbuf, local_sem.at[3])
    load_f.start()
    load_s = pltpu.make_async_copy(small, dens, local_sem.at[6])
    load_s.start()

    def ring(step):
        return lax.rem(me + step + NZ, NZ)

    def side(step):
        return lax.rem(gx + step + NG, NG)

    barrier = pltpu.get_barrier_semaphore()
    for dx in (0, -1, 1):
        for dz in (-1, 0, 1):
            if dx or dz:
                pl.semaphore_signal(barrier, inc=1, device_id=(ring(dz), side(dx)), device_id_type=MESH)

    def tell(level):
        for way in (-1, 1):
            pl.semaphore_signal(
                heard.at[level], inc=1, device_id=(ring(way * (1 << level)), gx), device_id_type=MESH
            )

    def hear(level):
        pl.semaphore_wait(heard.at[level], 2)

    for load in loads:
        load.wait()
    for h in range(2):
        for c in range(2):
            for x in range(XR):
                field[HALO + x, c, :, h * 128 : (h + 1) * 128] = stage[h, pl.ds(c * TL * XR + x, TL, stride=XR), :]

    pl.semaphore_wait(barrier, 8)
    tell(0)

    def row_copies(q):
        times = pl.ds(pl.multiple_of(q * TC, TC), TC)
        return [
            pltpu.make_async_remote_copy(
                src_ref=field.at[pl.ds(source, HALO), :, times, :],
                dst_ref=field.at[pl.ds(target, HALO), :, times, :],
                send_sem=xsend.at[q, way],
                recv_sem=xrecv.at[q, way],
                device_id=(me, side(dx)),
                device_id_type=MESH,
            )
            for way, (source, target, dx) in enumerate(((XR, 0, 1), (HALO, HALO + XR, -1)))
        ]

    for q in range(TL // TC):
        for copy in row_copies(q):
            copy.start()
    hear(0)
    tell(1)
    hear(1)
    tell(2)

    def column_copy(group, index, step, first, count):
        peer = ring(step)
        return pltpu.make_async_remote_copy(
            src_ref=sbuf.at[group, peer, pl.ds(first, count), :],
            dst_ref=rbuf.at[group, pl.ds(pl.multiple_of(me * TL, TL) + first, count), :],
            send_sem=asend.at[index, step],
            recv_sem=arecv.at[index, step],
            device_id=(peer, gx),
            device_id_type=MESH,
        )

    order = [s for k in range(8, 0, -1) for s in ((k, NZ - k) if k < 8 else (8,))]
    near = [step for step in order if min(step, NZ - step) <= 4]
    far = [step for step in order if min(step, NZ - step) > 4]
    messages = ((0, 0, 0, TL // 2, near), (0, 1, TL // 2, TL // 2, near), (0, 0, 0, TL, far), (1, 2, 0, TL, order))
    above = jnp.where(gx == 0, 0.0, 1.0).astype(F32)
    below = jnp.where(gx == NG - 1, 0.0, 1.0).astype(F32)

    def first_diffraction(q, carry):
        times = pl.ds(pl.multiple_of(q * TC, TC), TC)
        for copy in row_copies(q):
            copy.wait_recv()
        lane = lax.broadcasted_iota(jnp.int32, ((XR + 2 * HALO) * TC, 128), 1)
        slot = lax.broadcasted_iota(jnp.int32, (TC, 128), 1) // YC
        parts = []
        for c in range(2):
            halves = []
            for h in range(2):
                value = field[:, c, times, h * 128 : (h + 1) * 128]
                value = jnp.concatenate([value[:HALO] * above, value[HALO:-HALO], value[-HALO:] * below], axis=0)
                halves.append(value.reshape((XR + 2 * HALO) * TC, 128))
            parts.append(halves)
        parts = diffract(parts[0], parts[1], above, below, lane == 0, lane == 127)
        for h in range(2):
            for group in range(2):
                turned = []
                for s in range(8):
                    first = (group * HALO + s // 2) * TC
                    part = parts[h][s % 2][first : first + TC]
                    turned.append(pltpu.roll(part, YC * s, axis=1) if s else part)
                for jj in range(8):
                    piece = turned[0]
                    for s in range(1, 8):
                        piece = jnp.where(slot == (jj + s) % 8, turned[s], piece)
                    if jj:
                        piece = pltpu.roll(piece, 128 - YC * jj, axis=1)
                    sbuf[group, h * 8 + jj, times, :] = piece
        return carry

    half = TL // TC // 2
    for part, (group, index, first, count, steps) in enumerate(messages):
        if part < 2:
            lax.fori_loop(part * half, (part + 1) * half, first_diffraction, 0)
        if part == 2:
            hear(2)
        for step in steps:
            column_copy(group, index, step, first, count).start()
    mine = [
        pltpu.make_async_copy(
            sbuf.at[group, me], rbuf.at[group, pl.ds(pl.multiple_of(me * TL, TL), TL), :], local_sem.at[group]
        )
        for group in range(2)
    ]
    for copy in mine:
        copy.start()

    load_f.wait()
    load_s.wait()
    turn = dens[0:1, NY:]
    sine, cosine = sincos(turn)
    pair = jnp.concatenate([cosine, sine] * 4, axis=0) * (1.0 / NT)
    by_cos = jnp.dot(pair, fbuf[0], precision=lax.Precision.HIGHEST, preferred_element_type=F32)
    by_sin = jnp.dot(pair, fbuf[1], precision=lax.Precision.HIGHEST, preferred_element_type=F32)
    rows16 = lax.broadcasted_iota(jnp.int32, (16, NT), 0)
    for part, line in enumerate((by_cos[0:1] - by_sin[1:2], by_sin[0:1] + by_cos[1:2])):
        base = jnp.broadcast_to(line, (16, NT))
        for bit in range(4):
            base = jnp.where((rows16 >> bit) & 1 == 1, pltpu.roll(base, 1 << bit, axis=1), base)
        for block in range(NT // 16):
            high, low = split(pltpu.roll(base, 16 * block, axis=1) if block else base)
            for k in range(NT // 128):
                ch[k, 16 * block : 16 * block + 16, part * 128 : (part + 1) * 128] = high[:, k * 128 : (k + 1) * 128]
                cl[k, 16 * block : 16 * block + 16, part * 128 : (part + 1) * 128] = low[:, k * 128 : (k + 1) * 128]

    def tri_rows(block, carry):
        first = pl.multiple_of(block * 16, 16)
        row = lax.broadcasted_iota(jnp.int32, (16, NT), 0) + first
        col = lax.broadcasted_iota(jnp.int32, (16, NT), 1)
        tri[pl.ds(first, 16), :] = jnp.where(row < col, 1.0, 0.0).astype(BF16)
        return carry

    lax.fori_loop(0, NT // 16, tri_rows, 0)
    lane = lax.broadcasted_iota(jnp.int32, (YC, NY), 1)
    row = lax.broadcasted_iota(jnp.int32, (YC, NY), 0)
    wanted = lane == row + me * YC
    for x in range(XR):
        line = jnp.broadcast_to(dens[x : x + 1, :NY], (YC, NY))
        column = jnp.sum(jnp.where(wanted, line, 0.0), axis=1, keepdims=True)
        dcol[x * YC : (x + 1) * YC, :] = jnp.broadcast_to(column * (ionize_gain / NT), (YC, NT))
    load_w.wait()

    def kick(group):
        def rates(x, carry):
            first = pl.multiple_of(x * PAIR, PAIR)
            place = pl.ds(pl.multiple_of(x * YC, YC), YC)
            re = grid[pl.ds(first, YC), :]
            im = grid[pl.ds(first + YC, YC), :]
            intensity = re * re + im * im
            inten[place, :] = intensity
            high, low = split(dcol[place, :] * intensity * intensity)
            rh[place, :] = high
            rl[place, :] = low
            return carry

        lax.fori_loop(group * HALO, (group + 1) * HALO, rates, 0, unroll=True)
        cells = slice(group * CELLS // 2, (group + 1) * CELLS // 2)
        both = dot(jnp.concatenate([rh[cells, :], rl[cells, :]], axis=0), tri[...])
        plasma[cells, :] = both[: CELLS // 2] + both[CELLS // 2 :]

        def turn(x, carry):
            first = pl.multiple_of(x * PAIR, PAIR)
            place = pl.ds(pl.multiple_of(x * YC, YC), YC)
            re = grid[pl.ds(first, YC), :]
            im = grid[pl.ds(first + YC, YC), :]
            earlier = plasma[place, :]
            sine, cosine = sincos(kerr_gain * inten[place, :] - plasma_gain * earlier)
            amplitude = jnp.exp(-absorb_gain * earlier)
            sine = sine * amplitude
            cosine = cosine * amplitude
            high, low = split(re * cosine - im * sine)
            uh[pl.ds(first, YC), :] = high
            ul[pl.ds(first, YC), :] = low
            high, low = split(re * sine + im * cosine)
            uh[pl.ds(first + YC, YC), :] = high
            ul[pl.ds(first + YC, YC), :] = low
            return carry

        lax.fori_loop(group * HALO, (group + 1) * HALO, turn, 0, unroll=True)

    def disperse(group, chunk):
        rows = slice(group * OWN // 2, (group + 1) * OWN // 2)
        both = dot(jnp.concatenate([uh[rows, :], ul[rows, :]], axis=0), ch[chunk])
        value = both[: OWN // 2] + both[OWN // 2 :] + dot(uh[rows, :], cl[chunk])
        result = []
        for x in range(HALO):
            re = value[x * PAIR : x * PAIR + YC]
            im = value[x * PAIR + YC : (x + 1) * PAIR]
            result.append(re[:, :128] - im[:, 128:])
            result.append(re[:, 128:] + im[:, :128])
        return jnp.concatenate(result, axis=0)

    def halo_copy(index, source, first, dx, dz):
        return pltpu.make_async_remote_copy(
            src_ref=source,
            dst_ref=ext.at[pl.ds(first, source.shape[0]), :],
            send_sem=hsend.at[index],
            recv_sem=hrecv.at[index],
            device_id=(ring(dz), side(dx)),
            device_id_type=MESH,
        )

    def halo_copies(group):
        rows = pl.ds(group * 32, 32)
        towards = 2 * group - 1
        end = pl.ds(40 * group, 24)
        return [
            halo_copy(5 * group, ext.at[pl.ds(group * OWN // 2, OWN // 2), :], UP if group else DOWN, towards, 0),
            halo_copy(5 * group + 1, yhi.at[rows, :], LEFT + 32 * group, 0, 1),
            halo_copy(5 * group + 2, ylo.at[rows, :], RIGHT + 32 * group, 0, -1),
            halo_copy(5 * group + 3, yhi.at[end, :], (UP if group else DOWN) + HALO * PAIR, towards, 1),
            halo_copy(5 * group + 4, ylo.at[end, :], (UP if group else DOWN) + HALO * PAIR + 24, towards, -1),
        ]

    def split_rows(block, carry):
        place = pl.ds(pl.multiple_of(block * 16, 16), 16)
        high, low = split(ext[place, :])
        exth[place, :] = high
        extl[place, :] = low
        return carry

    low4 = lax.broadcasted_iota(jnp.int32, (8, NT), 0) < HALO
    for group in range(2):
        mine[group].wait()
        for g, index, first, count, steps in messages:
            if g == group:
                for step in steps:
                    column_copy(g, index, step, first, count).wait_recv()
        base = group * OWN // 2
        grid[base : base + OWN // 2, :] = rbuf[group].T
        kick(group)
        for chunk in range(NT // 128):
            ext[base : base + OWN // 2, chunk * 128 : (chunk + 1) * 128] = disperse(group, chunk)
        halo_copies(group)[0].start()
        for x in range(group * HALO, (group + 1) * HALO):
            first = x * PAIR
            ylo[8 * x : 8 * x + 8, :] = jnp.where(
                low4, ext[first : first + 8, :], pltpu.roll(ext[first + 16 : first + 24, :], 4, axis=0)
            )
            yhi[8 * x : 8 * x + 8, :] = jnp.where(
                low4, pltpu.roll(ext[first + 8 : first + 16, :], 4, axis=0), ext[first + 24 : first + 32, :]
            )
        for copy in halo_copies(group)[1:]:
            copy.start()

    lax.fori_loop(0, OWN // 16, split_rows, 0)
    both = dot(jnp.concatenate([wbuf[0, :, :OWN], wbuf[1, :, :OWN]], axis=0), exth[:OWN])
    grid[...] = both[:OWN] + both[OWN:] + dot(wbuf[0, :, :OWN], extl[:OWN])

    def shard_copy(group, step):
        peer = ring(step)
        return pltpu.make_async_remote_copy(
            src_ref=fin.at[group, pl.ds(pl.multiple_of(peer * TL, TL), TL), :],
            dst_ref=obuf.at[group, me],
            send_sem=bsend.at[group, step],
            recv_sem=brecv.at[group, step],
            device_id=(peer, gx),
            device_id_type=MESH,
        )

    mine = [
        pltpu.make_async_copy(
            fin.at[group, pl.ds(pl.multiple_of(me * TL, TL), TL), :], obuf.at[group, me], local_sem.at[group]
        )
        for group in range(2)
    ]
    for group in (1, 0):
        for index in (1, 2) if group else ():
            for g in range(2):
                halo_copies(g)[index].wait_recv()
        for index in (0, 3, 4):
            halo_copies(1 - group)[index].wait_recv()
        rows = slice(group * OWN // 2, (group + 1) * OWN // 2)
        first = OWN if group else UP
        lax.fori_loop(first // 16, (first + (UP - OWN if group else EXT - UP)) // 16, split_rows, 0)
        if group:
            grid[rows, :] += triple(wbuf[0, rows, OWN:UP], wbuf[1, rows, OWN:UP], exth[OWN:UP], extl[OWN:UP])
        else:
            for a, b in ((OWN, DOWN), (UP, EXT)):
                grid[rows, :] += triple(wbuf[0, rows, a:b], wbuf[1, rows, a:b], exth[a:b], extl[a:b])
        kick(group)
        for apart in (2, 1, 3, 0):
            chunk = lax.rem(lax.div(me, 4) + apart, 4)
            fin[group, pl.ds(pl.multiple_of(chunk * 128, 128), 128), :] = disperse(group, chunk).T
            for r in range(4):
                step = lax.rem(chunk * 4 + r - me + NZ, NZ)
                if apart:
                    shard_copy(group, step).start()
                else:

                    @pl.when(step != 0)
                    def _():
                        shard_copy(group, step).start()

        mine[group].start()

    for q in range(TL // TC):
        for copy in row_copies(q):
            copy.wait_send()
    for group, index, first, count, steps in messages:
        for step in steps:
            column_copy(group, index, step, first, count).wait_send()
    for group in range(2):
        for copy in halo_copies(group):
            copy.wait_send()

    slot = lax.broadcasted_iota(jnp.int32, (TL, 128), 1) // YC
    for group in (1, 0):
        mine[group].wait()
        for step in order:
            shard_copy(group, step).wait_recv()
        for h in range(2):
            turned = []
            for jj in range(8):
                part = obuf[group, h * 8 + jj]
                turned.append(pltpu.roll(part, YC * jj, axis=1) if jj else part)
            for s in range(8):
                piece = turned[0]
                for jj in range(1, 8):
                    piece = jnp.where(slot == (jj + s) % 8, turned[jj], piece)
                if s:
                    piece = pltpu.roll(piece, 128 - YC * s, axis=1)
                stage[h, pl.ds((s % 2) * TL * XR + group * HALO + s // 2, TL, stride=XR), :] = piece
    for h in range(2):
        out[:, h * 128 : (h + 1) * 128] = stage[h]
    for group in range(2):
        for step in order:
            shard_copy(group, step).wait_send()


def per_device(envelope, density_map, disp_phase):
    rows = 2 * TL * XR
    vmem = pl.BlockSpec(memory_space=pltpu.VMEM)
    anywhere = pl.BlockSpec(memory_space=pltpu.HBM)
    dma = pltpu.SemaphoreType.DMA
    result = pl.pallas_call(
        kernel,
        out_shape=jax.ShapeDtypeStruct((rows, NY), F32),
        in_specs=[anywhere] * 4,
        out_specs=vmem,
        scratch_shapes=[
            pltpu.VMEM((XR, NY + NT), F32),
            pltpu.VMEM((2, rows, 128), F32),
            pltpu.VMEM((XR + 2 * HALO, 2, TL, NY), F32),
            pltpu.VMEM((2, NZ, TL, 128), F32),
            pltpu.VMEM((2, NT, 128), F32),
            pltpu.VMEM((EXT, NT), F32),
            pltpu.VMEM((EXT, NT), BF16),
            pltpu.VMEM((EXT, NT), BF16),
            pltpu.VMEM((8 * XR, NT), F32),
            pltpu.VMEM((8 * XR, NT), F32),
            pltpu.VMEM((NT // 128, NT, 256), BF16),
            pltpu.VMEM((NT // 128, NT, 256), BF16),
            pltpu.VMEM((NT, NT), BF16),
            pltpu.VMEM((2, OWN, EXT), BF16),
            pltpu.VMEM((2, NT, NT), F32),
            pltpu.VMEM((CELLS, NT), F32),
            pltpu.VMEM((OWN, NT), F32),
            pltpu.VMEM((CELLS, NT), F32),
            pltpu.VMEM((CELLS, NT), BF16),
            pltpu.VMEM((CELLS, NT), BF16),
            pltpu.VMEM((CELLS, NT), F32),
            pltpu.VMEM((OWN, NT), BF16),
            pltpu.VMEM((OWN, NT), BF16),
            pltpu.VMEM((2, NT, 128), F32),
            pltpu.VMEM((2, NZ, TL, 128), F32),
            pltpu.SemaphoreType.REGULAR((3,)),
            dma((8,)),
            dma((TL // TC, 2)),
            dma((TL // TC, 2)),
            dma((3, NZ)),
            dma((3, NZ)),
            dma((10,)),
            dma((10,)),
            dma((2, NZ)),
            dma((2, NZ)),
        ],
        compiler_params=pltpu.CompilerParams(
            collective_id=0, has_side_effects=True, vmem_limit_bytes=53 * 1024 * 1024
        ),
        name="filament",
    )(
        envelope.reshape(rows, NY),
        jnp.concatenate([density_map, jnp.broadcast_to(disp_phase.reshape(1, NT), (XR, NT))], axis=1),
        jnp.asarray(diffraction_matrices()),
        jnp.asarray(fourier_matrices()),
    )
    return result.reshape(2, TL, XR, NY)


def solution(mesh):
    placed = (P(None, "ta", "gx", None), P("gx", None), P())
    return jax.shard_map(
        per_device, mesh=mesh, in_specs=placed, out_specs=P(None, "ta", "gx", None), check_vma=False
    )
```

```python
import functools
import math

import jax
import jax.numpy as jnp
import ml_dtypes
import numpy as np
from jax import lax
from jax.experimental import pallas as pl
from jax.experimental.pallas import tpu as pltpu
from jax.sharding import PartitionSpec as P

MESH = pl.DeviceIdType.MESH
F32 = jnp.float32
BF16 = jnp.bfloat16

STEPS = 2
NT = 512
NZ = 16
TL = NT // NZ
NG = 32
XR = 8
NY = 256
YC = NY // NZ
CELLS = XR * YC
OWN = 2 * CELLS
HALO = 4
TC = 8
PAIR = 2 * YC

LEFT = OWN
RIGHT = LEFT + 8 * XR
DOWN = RIGHT + 8 * XR
UP = DOWN + HALO * PAIR + 48
EXT = UP + HALO * PAIR + 48

diffract_step = 0.25
ionize_gain = 0.4
kerr_gain = 0.5
plasma_gain = 1.0
absorb_gain = 0.05


def row_cells():
    rows = []
    for x in range(XR):
        for c in range(2):
            for y in range(YC):
                rows.append((x, y, c))
    for base in (-HALO, YC):
        for x in range(XR):
            for c in range(2):
                for y in range(HALO):
                    rows.append((x, base + y, c))
    for xbase in (XR, -HALO):
        for x in range(HALO):
            for c in range(2):
                for y in range(YC):
                    rows.append((xbase + x, y, c))
        for ybase in (-HALO, YC):
            for x in range(3):
                for c in range(2):
                    for y in range(HALO):
                        rows.append((max(xbase, -3) + x, ybase + y, c))
    return rows


def diffraction_matrices():
    rows = row_cells()
    wide, high = YC + 2 * HALO, XR + 2 * HALO
    result = np.zeros((9, 2, OWN, EXT), ml_dtypes.bfloat16)
    for vx in range(3):
        for vy in range(3):
            inside = np.ones((high, wide), bool)
            if vx == 0:
                inside[:HALO] = False
            if vx == 2:
                inside[-HALO:] = False
            if vy == 0:
                inside[:, :HALO] = False
            if vy == 2:
                inside[:, -HALO:] = False
            count = high * wide
            lap = np.zeros((count, count))
            for x in range(high):
                for y in range(wide):
                    if not inside[x, y]:
                        continue
                    lap[x * wide + y, x * wide + y] = -4.0
                    for dx, dy in ((1, 0), (-1, 0), (0, 1), (0, -1)):
                        a, b = x + dx, y + dy
                        if 0 <= a < high and 0 <= b < wide and inside[a, b]:
                            lap[x * wide + y, a * wide + b] = 1.0
            own = [(x + HALO) * wide + y + HALO for x in range(XR) for y in range(YC)]
            power = np.eye(count)[own].astype(complex)
            total = power.copy()
            for n in range(1, 5):
                power = power @ lap * (1j * diffract_step / n)
                total = total + power
            place = {(x, y): i for i, (x, y) in enumerate((x, y) for x in range(XR) for y in range(YC))}
            matrix = np.zeros((OWN, EXT))
            for out_row, (x, y, c) in enumerate(rows[:OWN]):
                line = total[place[(x, y)]]
                for col, (a, b, d) in enumerate(rows):
                    value = line[(a + HALO) * wide + b + HALO]
                    if c == d:
                        matrix[out_row, col] = value.real
                    else:
                        matrix[out_row, col] = -value.imag if c == 0 else value.imag
            matrix = matrix.astype(np.float32)
            upper = matrix.astype(ml_dtypes.bfloat16)
            result[vx * 3 + vy, 0] = upper
            result[vx * 3 + vy, 1] = (matrix - upper.astype(np.float32)).astype(ml_dtypes.bfloat16)
    return result


def fourier_matrices():
    index = np.arange(NT)
    angles = (index[:, None] * index[None, :] % NT) * (2.0 * math.pi / NT)
    return np.stack([np.cos(angles), np.sin(angles)]).astype(np.float32)


def split(value):
    upper = value.astype(BF16)
    return upper, (value - upper.astype(F32)).astype(BF16)


def dot(a, b):
    return jnp.dot(a, b, preferred_element_type=F32)


def triple(ah, al, bh, bl):
    return dot(ah, bh) + dot(ah, bl) + dot(al, bh)


def sincos(angle):
    turns = jnp.floor(angle * (2.0 / math.pi) + 0.5)
    rest = ((angle - turns * 1.5703125) - turns * 4.837512969970703125e-4) - turns * 7.54978995489188216e-8
    quarter = turns.astype(jnp.int32)
    z = rest * rest
    sine = ((-1.9515295891e-4 * z + 8.3321608736e-3) * z - 1.6666654611e-1) * (z * rest) + rest
    cosine = ((2.443315711809948e-5 * z - 1.388731625493765e-3) * z + 4.166664568298827e-2) * (z * z) + (1.0 - 0.5 * z)
    odd = (quarter & 1) == 1
    a = jnp.where(odd, cosine, sine)
    b = jnp.where(odd, sine, cosine)
    a = jnp.where((quarter & 2) == 2, -a, a)
    b = jnp.where(((quarter + 1) & 2) == 2, -b, b)
    return a, b


def lap_powers(halves, above, below, first, last):
    result = []
    for number in range(1, HALO + 1):
        centre = [part[TC:-TC] for part in halves]
        rows = centre[0].shape[0]
        up = [pltpu.roll(part, 1, axis=1) for part in centre]
        down = [pltpu.roll(part, 127, axis=1) for part in centre]
        beside = [
            jnp.where(first[:rows], 0.0, up[0]) + jnp.where(last[:rows], down[1], down[0]),
            jnp.where(first[:rows], up[0], up[1]) + jnp.where(last[:rows], 0.0, down[1]),
        ]
        rest = (HALO - number) * TC
        out = []
        for part, mid, across in zip(halves, centre, beside):
            lapped = (part[2 * TC :] + part[: -2 * TC]) + (across - 4.0 * mid)
            if rest:
                lapped = jnp.concatenate([lapped[:rest] * above, lapped[rest:-rest], lapped[-rest:] * below], axis=0)
            out.append(lapped)
        halves = out
        result.append([part[rest:-rest] if rest else part for part in halves])
    return result


def diffract(re, im, above, below, first, last):
    edge = HALO * TC
    by_re = lap_powers(re, above, below, first, last)
    by_im = lap_powers(im, above, below, first, last)
    a1, a2, a3, a4 = (diffract_step**n / math.factorial(n) for n in range(1, 5))
    out = []
    for h in range(2):
        r1, r2, r3, r4 = (by_re[n][h] for n in range(4))
        i1, i2, i3, i4 = (by_im[n][h] for n in range(4))
        out.append(
            (
                re[h][edge:-edge] - a1 * i1 - a2 * r2 + a3 * i3 + a4 * r4,
                im[h][edge:-edge] + a1 * r1 - a2 * i2 - a3 * r3 + a4 * i4,
            )
        )
    return out


def kernel(
    env, small, wmat, fourier, out,
    dens, stage, field, sbuf, rbuf, ext, exth, extl, ylo, yhi, ch, cl, tri, wbuf, fbuf, dcol,
    grid, inten, rh, rl, plasma, uh, ul, fin, obuf,
    heard, local_sem, xsend, xrecv, asend, arecv, hsend, hrecv, bsend, brecv,
):
    me = lax.axis_index("ta")
    gx = lax.axis_index("gx")

    loads = [
        pltpu.make_async_copy(env.at[:, pl.ds(h * 128, 128)], stage.at[h], local_sem.at[4 + h]) for h in range(2)
    ]
    for load in loads:
        load.start()
    variant = (lax.div(gx + NG - 2, NG - 1) + lax.div(gx, NG - 1)) * 3 + lax.div(me + NZ - 2, NZ - 1) + lax.div(me, NZ - 1)
    load_w = pltpu.make_async_copy(wmat.at[variant], wbuf, local_sem.at[2])
    load_w.start()
    load_f = pltpu.make_async_copy(fourier, fbuf, local_sem.at[3])
    load_f.start()
    load_s = pltpu.make_async_copy(small, dens, local_sem.at[6])
    load_s.start()

    def ring(step):
        return lax.rem(me + step + NZ, NZ)

    def side(step):
        return lax.rem(gx + step + NG, NG)

    barrier = pltpu.get_barrier_semaphore()
    for dx in (0, -1, 1):
        for dz in (-1, 0, 1):
            if dx or dz:
                pl.semaphore_signal(barrier, inc=1, device_id=(ring(dz), side(dx)), device_id_type=MESH)

    def tell(level):
        for way in (-1, 1):
            pl.semaphore_signal(
                heard.at[level], inc=1, device_id=(ring(way * (1 << level)), gx), device_id_type=MESH
            )

    def hear(level):
        pl.semaphore_wait(heard.at[level], 2)

    for load in loads:
        load.wait()
    for h in range(2):
        for c in range(2):
            for x in range(XR):
                field[HALO + x, c, :, h * 128 : (h + 1) * 128] = stage[h, pl.ds(c * TL * XR + x, TL, stride=XR), :]

    pl.semaphore_wait(barrier, 8)
    tell(0)

    def row_copies(q):
        times = pl.ds(pl.multiple_of(q * TC, TC), TC)
        return [
            pltpu.make_async_remote_copy(
                src_ref=field.at[pl.ds(source, HALO), :, times, :],
                dst_ref=field.at[pl.ds(target, HALO), :, times, :],
                send_sem=xsend.at[q, way],
                recv_sem=xrecv.at[q, way],
                device_id=(me, side(dx)),
                device_id_type=MESH,
            )
            for way, (source, target, dx) in enumerate(((XR, 0, 1), (HALO, HALO + XR, -1)))
        ]

    for q in range(TL // TC):
        for copy in row_copies(q):
            copy.start()
    hear(0)
    tell(1)
    hear(1)
    tell(2)

    def column_copy(group, index, step, first, count):
        peer = ring(step)
        return pltpu.make_async_remote_copy(
            src_ref=sbuf.at[group, peer, pl.ds(first, count), :],
            dst_ref=rbuf.at[group, pl.ds(pl.multiple_of(me * TL, TL) + first, count), :],
            send_sem=asend.at[index, step],
            recv_sem=arecv.at[index, step],
            device_id=(peer, gx),
            device_id_type=MESH,
        )

    order = [s for k in range(8, 0, -1) for s in ((k, NZ - k) if k < 8 else (8,))]
    near = [step for step in order if min(step, NZ - step) <= 4]
    far = [step for step in order if min(step, NZ - step) > 4]
    messages = ((0, 0, 0, TL // 2, near), (0, 1, TL // 2, TL // 2, near), (0, 0, 0, TL, far), (1, 2, 0, TL, order))
    above = jnp.where(gx == 0, 0.0, 1.0).astype(F32)
    below = jnp.where(gx == NG - 1, 0.0, 1.0).astype(F32)

    def first_diffraction(q, carry):
        times = pl.ds(pl.multiple_of(q * TC, TC), TC)
        for copy in row_copies(q):
            copy.wait_recv()
        lane = lax.broadcasted_iota(jnp.int32, ((XR + 2 * HALO) * TC, 128), 1)
        slot = lax.broadcasted_iota(jnp.int32, (TC, 128), 1) // YC
        parts = []
        for c in range(2):
            halves = []
            for h in range(2):
                value = field[:, c, times, h * 128 : (h + 1) * 128]
                value = jnp.concatenate([value[:HALO] * above, value[HALO:-HALO], value[-HALO:] * below], axis=0)
                halves.append(value.reshape((XR + 2 * HALO) * TC, 128))
            parts.append(halves)
        parts = diffract(parts[0], parts[1], above, below, lane == 0, lane == 127)
        for h in range(2):
            for group in range(2):
                turned = []
                for s in range(8):
                    first = (group * HALO + s // 2) * TC
                    part = parts[h][s % 2][first : first + TC]
                    turned.append(pltpu.roll(part, YC * s, axis=1) if s else part)
                for jj in range(8):
                    piece = turned[0]
                    for s in range(1, 8):
                        piece = jnp.where(slot == (jj + s) % 8, turned[s], piece)
                    if jj:
                        piece = pltpu.roll(piece, 128 - YC * jj, axis=1)
                    sbuf[group, h * 8 + jj, times, :] = piece
        return carry

    half = TL // TC // 2
    for part, (group, index, first, count, steps) in enumerate(messages):
        if part < 2:
            lax.fori_loop(part * half, (part + 1) * half, first_diffraction, 0)
        if part == 2:
            hear(2)
        for step in steps:
            column_copy(group, index, step, first, count).start()
    mine = [
        pltpu.make_async_copy(
            sbuf.at[group, me], rbuf.at[group, pl.ds(pl.multiple_of(me * TL, TL), TL), :], local_sem.at[group]
        )
        for group in range(2)
    ]
    for copy in mine:
        copy.start()

    load_f.wait()
    load_s.wait()
    turn = dens[0:1, NY:]
    sine, cosine = sincos(turn)
    pair = jnp.concatenate([cosine, sine] * 4, axis=0) * (1.0 / NT)
    by_cos = jnp.dot(pair, fbuf[0], precision=lax.Precision.HIGHEST, preferred_element_type=F32)
    by_sin = jnp.dot(pair, fbuf[1], precision=lax.Precision.HIGHEST, preferred_element_type=F32)
    rows16 = lax.broadcasted_iota(jnp.int32, (16, NT), 0)
    for part, line in enumerate((by_cos[0:1] - by_sin[1:2], by_sin[0:1] + by_cos[1:2])):
        base = jnp.broadcast_to(line, (16, NT))
        for bit in range(4):
            base = jnp.where((rows16 >> bit) & 1 == 1, pltpu.roll(base, 1 << bit, axis=1), base)
        for block in range(NT // 16):
            high, low = split(pltpu.roll(base, 16 * block, axis=1) if block else base)
            for k in range(NT // 128):
                ch[k, 16 * block : 16 * block + 16, part * 128 : (part + 1) * 128] = high[:, k * 128 : (k + 1) * 128]
                cl[k, 16 * block : 16 * block + 16, part * 128 : (part + 1) * 128] = low[:, k * 128 : (k + 1) * 128]

    def tri_rows(block, carry):
        first = pl.multiple_of(block * 16, 16)
        row = lax.broadcasted_iota(jnp.int32, (16, NT), 0) + first
        col = lax.broadcasted_iota(jnp.int32, (16, NT), 1)
        tri[pl.ds(first, 16), :] = jnp.where(row < col, 1.0, 0.0).astype(BF16)
        return carry

    lax.fori_loop(0, NT // 16, tri_rows, 0)
    lane = lax.broadcasted_iota(jnp.int32, (YC, NY), 1)
    row = lax.broadcasted_iota(jnp.int32, (YC, NY), 0)
    wanted = lane == row + me * YC
    for x in range(XR):
        line = jnp.broadcast_to(dens[x : x + 1, :NY], (YC, NY))
        column = jnp.sum(jnp.where(wanted, line, 0.0), axis=1, keepdims=True)
        dcol[x * YC : (x + 1) * YC, :] = jnp.broadcast_to(column * (ionize_gain / NT), (YC, NT))
    load_w.wait()

    def kick(group):
        def rates(x, carry):
            first = pl.multiple_of(x * PAIR, PAIR)
            place = pl.ds(pl.multiple_of(x * YC, YC), YC)
            re = grid[pl.ds(first, YC), :]
            im = grid[pl.ds(first + YC, YC), :]
            intensity = re * re + im * im
            inten[place, :] = intensity
            high, low = split(dcol[place, :] * intensity * intensity)
            rh[place, :] = high
            rl[place, :] = low
            return carry

        lax.fori_loop(group * HALO, (group + 1) * HALO, rates, 0, unroll=True)
        cells = slice(group * CELLS // 2, (group + 1) * CELLS // 2)
        both = dot(jnp.concatenate([rh[cells, :], rl[cells, :]], axis=0), tri[...])
        plasma[cells, :] = both[: CELLS // 2] + both[CELLS // 2 :]

        def turn(x, carry):
            first = pl.multiple_of(x * PAIR, PAIR)
            place = pl.ds(pl.multiple_of(x * YC, YC), YC)
            re = grid[pl.ds(first, YC), :]
            im = grid[pl.ds(first + YC, YC), :]
            earlier = plasma[place, :]
            sine, cosine = sincos(kerr_gain * inten[place, :] - plasma_gain * earlier)
            amplitude = jnp.exp(-absorb_gain * earlier)
            sine = sine * amplitude
            cosine = cosine * amplitude
            high, low = split(re * cosine - im * sine)
            uh[pl.ds(first, YC), :] = high
            ul[pl.ds(first, YC), :] = low
            high, low = split(re * sine + im * cosine)
            uh[pl.ds(first + YC, YC), :] = high
            ul[pl.ds(first + YC, YC), :] = low
            return carry

        lax.fori_loop(group * HALO, (group + 1) * HALO, turn, 0, unroll=True)

    def disperse(group, chunk):
        rows = slice(group * OWN // 2, (group + 1) * OWN // 2)
        both = dot(jnp.concatenate([uh[rows, :], ul[rows, :]], axis=0), ch[chunk])
        value = both[: OWN // 2] + both[OWN // 2 :] + dot(uh[rows, :], cl[chunk])
        result = []
        for x in range(HALO):
            re = value[x * PAIR : x * PAIR + YC]
            im = value[x * PAIR + YC : (x + 1) * PAIR]
            result.append(re[:, :128] - im[:, 128:])
            result.append(re[:, 128:] + im[:, :128])
        return jnp.concatenate(result, axis=0)

    def halo_copy(index, source, first, dx, dz):
        return pltpu.make_async_remote_copy(
            src_ref=source,
            dst_ref=ext.at[pl.ds(first, source.shape[0]), :],
            send_sem=hsend.at[index],
            recv_sem=hrecv.at[index],
            device_id=(ring(dz), side(dx)),
            device_id_type=MESH,
        )

    def halo_copies(group):
        rows = pl.ds(group * 32, 32)
        towards = 2 * group - 1
        end = pl.ds(40 * group, 24)
        return [
            halo_copy(5 * group, ext.at[pl.ds(group * OWN // 2, OWN // 2), :], UP if group else DOWN, towards, 0),
            halo_copy(5 * group + 1, yhi.at[rows, :], LEFT + 32 * group, 0, 1),
            halo_copy(5 * group + 2, ylo.at[rows, :], RIGHT + 32 * group, 0, -1),
            halo_copy(5 * group + 3, yhi.at[end, :], (UP if group else DOWN) + HALO * PAIR, towards, 1),
            halo_copy(5 * group + 4, ylo.at[end, :], (UP if group else DOWN) + HALO * PAIR + 24, towards, -1),
        ]

    def split_rows(block, carry):
        place = pl.ds(pl.multiple_of(block * 16, 16), 16)
        high, low = split(ext[place, :])
        exth[place, :] = high
        extl[place, :] = low
        return carry

    low4 = lax.broadcasted_iota(jnp.int32, (8, NT), 0) < HALO
    for group in range(2):
        mine[group].wait()
        for g, index, first, count, steps in messages:
            if g == group:
                for step in steps:
                    column_copy(g, index, step, first, count).wait_recv()
        base = group * OWN // 2
        grid[base : base + OWN // 2, :] = rbuf[group].T
        kick(group)
        for chunk in range(NT // 128):
            ext[base : base + OWN // 2, chunk * 128 : (chunk + 1) * 128] = disperse(group, chunk)
        for x in range(group * HALO, (group + 1) * HALO):
            first = x * PAIR
            ylo[8 * x : 8 * x + 8, :] = jnp.where(
                low4, ext[first : first + 8, :], pltpu.roll(ext[first + 16 : first + 24, :], 4, axis=0)
            )
            yhi[8 * x : 8 * x + 8, :] = jnp.where(
                low4, pltpu.roll(ext[first + 8 : first + 16, :], 4, axis=0), ext[first + 24 : first + 32, :]
            )
        for index in (1, 2, 0, 3, 4):
            halo_copies(group)[index].start()

    lax.fori_loop(0, OWN // 16, split_rows, 0)
    both = dot(jnp.concatenate([wbuf[0, :, :OWN], wbuf[1, :, :OWN]], axis=0), exth[:OWN])
    grid[...] = both[:OWN] + both[OWN:] + dot(wbuf[0, :, :OWN], extl[:OWN])

    def shard_copy(group, step):
        peer = ring(step)
        return pltpu.make_async_remote_copy(
            src_ref=fin.at[group, pl.ds(pl.multiple_of(peer * TL, TL), TL), :],
            dst_ref=obuf.at[group, me],
            send_sem=bsend.at[group, step],
            recv_sem=brecv.at[group, step],
            device_id=(peer, gx),
            device_id_type=MESH,
        )

    mine = [
        pltpu.make_async_copy(
            fin.at[group, pl.ds(pl.multiple_of(me * TL, TL), TL), :], obuf.at[group, me], local_sem.at[group]
        )
        for group in range(2)
    ]
    for group in (1, 0):
        for index in (1, 2) if group else ():
            for g in range(2):
                halo_copies(g)[index].wait_recv()
        for index in (0, 3, 4):
            halo_copies(1 - group)[index].wait_recv()
        rows = slice(group * OWN // 2, (group + 1) * OWN // 2)
        first = OWN if group else UP
        lax.fori_loop(first // 16, (first + (UP - OWN if group else EXT - UP)) // 16, split_rows, 0)
        if group:
            grid[rows, :] += triple(wbuf[0, rows, OWN:UP], wbuf[1, rows, OWN:UP], exth[OWN:UP], extl[OWN:UP])
        else:
            for a, b in ((OWN, DOWN), (UP, EXT)):
                grid[rows, :] += triple(wbuf[0, rows, a:b], wbuf[1, rows, a:b], exth[a:b], extl[a:b])
        kick(group)
        for apart in (2, 1, 3, 0):
            chunk = lax.rem(lax.div(me, 4) + apart, 4)
            fin[group, pl.ds(pl.multiple_of(chunk * 128, 128), 128), :] = disperse(group, chunk).T
            for turn in (0, 1, 3, 2):
                if apart or turn:
                    peer = chunk * 4 + lax.rem(me + turn, 4)
                    shard_copy(group, lax.rem(peer - me + NZ, NZ)).start()
        mine[group].start()

    for q in range(TL // TC):
        for copy in row_copies(q):
            copy.wait_send()
    for group, index, first, count, steps in messages:
        for step in steps:
            column_copy(group, index, step, first, count).wait_send()
    for group in range(2):
        for copy in halo_copies(group):
            copy.wait_send()

    slot = lax.broadcasted_iota(jnp.int32, (TL, 128), 1) // YC
    for group in (1, 0):
        mine[group].wait()
        for step in order:
            shard_copy(group, step).wait_recv()
        for h in range(2):
            turned = []
            for jj in range(8):
                part = obuf[group, h * 8 + jj]
                turned.append(pltpu.roll(part, YC * jj, axis=1) if jj else part)
            for s in range(8):
                piece = turned[0]
                for jj in range(1, 8):
                    piece = jnp.where(slot == (jj + s) % 8, turned[jj], piece)
                if s:
                    piece = pltpu.roll(piece, 128 - YC * s, axis=1)
                stage[h, pl.ds((s % 2) * TL * XR + group * HALO + s // 2, TL, stride=XR), :] = piece
    for h in range(2):
        out[:, h * 128 : (h + 1) * 128] = stage[h]
    for group in range(2):
        for step in order:
            shard_copy(group, step).wait_send()


def per_device(envelope, density_map, disp_phase):
    rows = 2 * TL * XR
    vmem = pl.BlockSpec(memory_space=pltpu.VMEM)
    anywhere = pl.BlockSpec(memory_space=pltpu.HBM)
    dma = pltpu.SemaphoreType.DMA
    result = pl.pallas_call(
        kernel,
        out_shape=jax.ShapeDtypeStruct((rows, NY), F32),
        in_specs=[anywhere] * 4,
        out_specs=vmem,
        scratch_shapes=[
            pltpu.VMEM((XR, NY + NT), F32),
            pltpu.VMEM((2, rows, 128), F32),
            pltpu.VMEM((XR + 2 * HALO, 2, TL, NY), F32),
            pltpu.VMEM((2, NZ, TL, 128), F32),
            pltpu.VMEM((2, NT, 128), F32),
            pltpu.VMEM((EXT, NT), F32),
            pltpu.VMEM((EXT, NT), BF16),
            pltpu.VMEM((EXT, NT), BF16),
            pltpu.VMEM((8 * XR, NT), F32),
            pltpu.VMEM((8 * XR, NT), F32),
            pltpu.VMEM((NT // 128, NT, 256), BF16),
            pltpu.VMEM((NT // 128, NT, 256), BF16),
            pltpu.VMEM((NT, NT), BF16),
            pltpu.VMEM((2, OWN, EXT), BF16),
            pltpu.VMEM((2, NT, NT), F32),
            pltpu.VMEM((CELLS, NT), F32),
            pltpu.VMEM((OWN, NT), F32),
            pltpu.VMEM((CELLS, NT), F32),
            pltpu.VMEM((CELLS, NT), BF16),
            pltpu.VMEM((CELLS, NT), BF16),
            pltpu.VMEM((CELLS, NT), F32),
            pltpu.VMEM((OWN, NT), BF16),
            pltpu.VMEM((OWN, NT), BF16),
            pltpu.VMEM((2, NT, 128), F32),
            pltpu.VMEM((2, NZ, TL, 128), F32),
            pltpu.SemaphoreType.REGULAR((3,)),
            dma((8,)),
            dma((TL // TC, 2)),
            dma((TL // TC, 2)),
            dma((3, NZ)),
            dma((3, NZ)),
            dma((10,)),
            dma((10,)),
            dma((2, NZ)),
            dma((2, NZ)),
        ],
        compiler_params=pltpu.CompilerParams(
            collective_id=0, has_side_effects=True, vmem_limit_bytes=53 * 1024 * 1024
        ),
        name="filament",
    )(
        envelope.reshape(rows, NY),
        jnp.concatenate([density_map, jnp.broadcast_to(disp_phase.reshape(1, NT), (XR, NT))], axis=1),
        jnp.asarray(diffraction_matrices()),
        jnp.asarray(fourier_matrices()),
    )
    return result.reshape(2, TL, XR, NY)


def solution(mesh):
    placed = (P(None, "ta", "gx", None), P("gx", None), P())
    return jax.shard_map(
        per_device, mesh=mesh, in_specs=placed, out_specs=P(None, "ta", "gx", None), check_vma=False
    )
```

```python
import functools
import math

import jax
import jax.numpy as jnp
import ml_dtypes
import numpy as np
from jax import lax
from jax.experimental import pallas as pl
from jax.experimental.pallas import tpu as pltpu
from jax.sharding import PartitionSpec as P

MESH = pl.DeviceIdType.MESH
F32 = jnp.float32
BF16 = jnp.bfloat16

STEPS = 2
NT = 512
NZ = 16
TL = NT // NZ
NG = 32
XR = 8
NY = 256
YC = NY // NZ
CELLS = XR * YC
OWN = 2 * CELLS
HALO = 4
TC = 8
PAIR = 2 * YC

LEFT = OWN
RIGHT = LEFT + 8 * XR
DOWN = RIGHT + 8 * XR
UP = DOWN + HALO * PAIR + 48
EXT = UP + HALO * PAIR + 48

diffract_step = 0.25
ionize_gain = 0.4
kerr_gain = 0.5
plasma_gain = 1.0
absorb_gain = 0.05


def row_cells():
    rows = []
    for x in range(XR):
        for c in range(2):
            for y in range(YC):
                rows.append((x, y, c))
    for base in (-HALO, YC):
        for x in range(XR):
            for c in range(2):
                for y in range(HALO):
                    rows.append((x, base + y, c))
    for xbase in (XR, -HALO):
        for x in range(HALO):
            for c in range(2):
                for y in range(YC):
                    rows.append((xbase + x, y, c))
        for ybase in (-HALO, YC):
            for x in range(3):
                for c in range(2):
                    for y in range(HALO):
                        rows.append((max(xbase, -3) + x, ybase + y, c))
    return rows


def diffraction_matrices():
    rows = row_cells()
    wide, high = YC + 2 * HALO, XR + 2 * HALO
    result = np.zeros((9, 2, OWN, EXT), ml_dtypes.bfloat16)
    for vx in range(3):
        for vy in range(3):
            inside = np.ones((high, wide), bool)
            if vx == 0:
                inside[:HALO] = False
            if vx == 2:
                inside[-HALO:] = False
            if vy == 0:
                inside[:, :HALO] = False
            if vy == 2:
                inside[:, -HALO:] = False
            count = high * wide
            lap = np.zeros((count, count))
            for x in range(high):
                for y in range(wide):
                    if not inside[x, y]:
                        continue
                    lap[x * wide + y, x * wide + y] = -4.0
                    for dx, dy in ((1, 0), (-1, 0), (0, 1), (0, -1)):
                        a, b = x + dx, y + dy
                        if 0 <= a < high and 0 <= b < wide and inside[a, b]:
                            lap[x * wide + y, a * wide + b] = 1.0
            own = [(x + HALO) * wide + y + HALO for x in range(XR) for y in range(YC)]
            power = np.eye(count)[own].astype(complex)
            total = power.copy()
            for n in range(1, 5):
                power = power @ lap * (1j * diffract_step / n)
                total = total + power
            place = {(x, y): i for i, (x, y) in enumerate((x, y) for x in range(XR) for y in range(YC))}
            matrix = np.zeros((OWN, EXT))
            for out_row, (x, y, c) in enumerate(rows[:OWN]):
                line = total[place[(x, y)]]
                for col, (a, b, d) in enumerate(rows):
                    value = line[(a + HALO) * wide + b + HALO]
                    if c == d:
                        matrix[out_row, col] = value.real
                    else:
                        matrix[out_row, col] = -value.imag if c == 0 else value.imag
            matrix = matrix.astype(np.float32)
            upper = matrix.astype(ml_dtypes.bfloat16)
            result[vx * 3 + vy, 0] = upper
            result[vx * 3 + vy, 1] = (matrix - upper.astype(np.float32)).astype(ml_dtypes.bfloat16)
    return result


def fourier_matrices():
    index = np.arange(NT)
    angles = (index[:, None] * index[None, :] % NT) * (2.0 * math.pi / NT)
    return np.stack([np.cos(angles), np.sin(angles)]).astype(np.float32)


def split(value):
    upper = value.astype(BF16)
    return upper, (value - upper.astype(F32)).astype(BF16)


def dot(a, b):
    return jnp.dot(a, b, preferred_element_type=F32)


def triple(ah, al, bh, bl):
    return dot(ah, bh) + dot(ah, bl) + dot(al, bh)


def sincos(angle):
    turns = jnp.floor(angle * (2.0 / math.pi) + 0.5)
    rest = ((angle - turns * 1.5703125) - turns * 4.837512969970703125e-4) - turns * 7.54978995489188216e-8
    quarter = turns.astype(jnp.int32)
    z = rest * rest
    sine = ((-1.9515295891e-4 * z + 8.3321608736e-3) * z - 1.6666654611e-1) * (z * rest) + rest
    cosine = ((2.443315711809948e-5 * z - 1.388731625493765e-3) * z + 4.166664568298827e-2) * (z * z) + (1.0 - 0.5 * z)
    odd = (quarter & 1) == 1
    a = jnp.where(odd, cosine, sine)
    b = jnp.where(odd, sine, cosine)
    a = jnp.where((quarter & 2) == 2, -a, a)
    b = jnp.where(((quarter + 1) & 2) == 2, -b, b)
    return a, b


def lap(before, row, after, first, last):
    up = [pltpu.roll(part, 1, axis=1) for part in row]
    down = [pltpu.roll(part, 127, axis=1) for part in row]
    beside = (
        jnp.where(first, 0.0, up[0]) + jnp.where(last, down[1], down[0]),
        jnp.where(first, up[0], up[1]) + jnp.where(last, 0.0, down[1]),
    )
    return [(before[h] + after[h]) + (beside[h] - 4.0 * row[h]) for h in range(2)]


def diffract(load, above, below, first, last):
    a1, a2, a3, a4 = (diffract_step**n / math.factorial(n) for n in range(1, 5))
    total = XR + 2 * HALO
    rows = [[{}, {}] for _ in range(HALO + 1)]

    def masked(row, x):
        factor = above if x < HALO else below if x >= HALO + XR else None
        return row if factor is None else [part * factor for part in row]

    for x in range(total):
        for c in range(2):
            rows[0][c][x] = masked(load(x, c), x)
        for n in range(1, HALO + 1):
            at = x - n
            if n <= at < total - n:
                for c in range(2):
                    lower = rows[n - 1][c]
                    rows[n][c][at] = masked(lap(lower[at - 1], lower[at], lower[at + 1], first, last), at)
        at = x - HALO
        if HALO <= at < HALO + XR:
            out = []
            for c, sign in ((0, 1.0), (1, -1.0)):
                mine = [rows[n][c][at] for n in range(HALO + 1)]
                other = [rows[n][1 - c][at] for n in range(HALO + 1)]
                out.append(
                    [
                        (mine[0][h] - a2 * mine[2][h] + a4 * mine[4][h])
                        + (sign * a3 * other[3][h] - sign * a1 * other[1][h])
                        for h in range(2)
                    ]
                )
            yield out


def kernel(
    env, small, wmat, fourier, out,
    dens, stage, field, sbuf, rbuf, ext, exth, extl, ylo, yhi, ch, cl, tri, wbuf, fbuf, dcol,
    grid, inten, rh, rl, plasma, uh, ul, fin, obuf,
    heard, local_sem, xsend, xrecv, asend, arecv, hsend, hrecv, bsend, brecv,
):
    me = lax.axis_index("ta")
    gx = lax.axis_index("gx")

    loads = [
        pltpu.make_async_copy(env.at[:, pl.ds(h * 128, 128)], stage.at[h], local_sem.at[4 + h]) for h in range(2)
    ]
    for load in loads:
        load.start()
    variant = (lax.div(gx + NG - 2, NG - 1) + lax.div(gx, NG - 1)) * 3 + lax.div(me + NZ - 2, NZ - 1) + lax.div(me, NZ - 1)
    load_w = pltpu.make_async_copy(wmat.at[variant], wbuf, local_sem.at[2])
    load_w.start()
    load_f = pltpu.make_async_copy(fourier, fbuf, local_sem.at[3])
    load_f.start()
    load_s = pltpu.make_async_copy(small, dens, local_sem.at[6])
    load_s.start()

    def ring(step):
        return lax.rem(me + step + NZ, NZ)

    def side(step):
        return lax.rem(gx + step + NG, NG)

    barrier = pltpu.get_barrier_semaphore()
    for dx in (0, -1, 1):
        for dz in (-1, 0, 1):
            if dx or dz:
                pl.semaphore_signal(barrier, inc=1, device_id=(ring(dz), side(dx)), device_id_type=MESH)

    def tell(level):
        for way in (-1, 1):
            pl.semaphore_signal(
                heard.at[level], inc=1, device_id=(ring(way * (1 << level)), gx), device_id_type=MESH
            )

    def hear(level):
        pl.semaphore_wait(heard.at[level], 2)

    pl.semaphore_wait(barrier, 8)
    tell(0)

    for load in loads:
        load.wait()
    for h in range(2):
        for c in range(2):
            for x in range(XR):
                field[HALO + x, c, :, h * 128 : (h + 1) * 128] = stage[h, pl.ds(c * TL * XR + x, TL, stride=XR), :]


    def row_copies(q):
        times = pl.ds(pl.multiple_of(q * TC, TC), TC)
        return [
            pltpu.make_async_remote_copy(
                src_ref=field.at[pl.ds(source, HALO), :, times, :],
                dst_ref=field.at[pl.ds(target, HALO), :, times, :],
                send_sem=xsend.at[q, way],
                recv_sem=xrecv.at[q, way],
                device_id=(me, side(dx)),
                device_id_type=MESH,
            )
            for way, (source, target, dx) in enumerate(((XR, 0, 1), (HALO, HALO + XR, -1)))
        ]

    for q in range(TL // TC):
        for copy in row_copies(q):
            copy.start()
    hear(0)
    tell(1)
    hear(1)
    tell(2)

    def column_copy(group, index, step, first, count):
        peer = ring(step)
        return pltpu.make_async_remote_copy(
            src_ref=sbuf.at[group, peer, pl.ds(first, count), :],
            dst_ref=rbuf.at[group, pl.ds(pl.multiple_of(me * TL, TL) + first, count), :],
            send_sem=asend.at[index, step],
            recv_sem=arecv.at[index, step],
            device_id=(peer, gx),
            device_id_type=MESH,
        )

    order = [s for k in range(8, 0, -1) for s in ((k, NZ - k) if k < 8 else (8,))]
    near = [step for step in order if min(step, NZ - step) <= 4]
    far = [step for step in order if min(step, NZ - step) > 4]
    messages = ((0, 0, 0, TL // 2, near), (0, 1, TL // 2, TL // 2, near), (0, 0, 0, TL, far), (1, 2, 0, TL, order))
    above = jnp.where(gx == 0, 0.0, 1.0).astype(F32)
    below = jnp.where(gx == NG - 1, 0.0, 1.0).astype(F32)

    def first_diffraction(q, carry):
        times = pl.ds(pl.multiple_of(q * TC, TC), TC)
        for copy in row_copies(q):
            copy.wait_recv()
        lane = lax.broadcasted_iota(jnp.int32, (TC, 128), 1)
        slot = lane // YC

        def load(x, c):
            return [field[x, c, times, h * 128 : (h + 1) * 128] for h in range(2)]

        turned = []
        for x, parts in enumerate(diffract(load, above, below, lane == 0, lane == 127)):
            for c in range(2):
                s = 2 * (x % HALO) + c
                turned.append([pltpu.roll(part, YC * s, axis=1) if s else part for part in parts[c]])
            if len(turned) == 2 * HALO:
                for h in range(2):
                    for jj in range(8):
                        piece = turned[0][h]
                        for s in range(1, 8):
                            piece = jnp.where(slot == (jj + s) % 8, turned[s][h], piece)
                        if jj:
                            piece = pltpu.roll(piece, 128 - YC * jj, axis=1)
                        sbuf[x // HALO, h * 8 + jj, times, :] = piece
                turned = []
        return carry

    half = TL // TC // 2
    for part, (group, index, first, count, steps) in enumerate(messages):
        if part < 2:
            lax.fori_loop(part * half, (part + 1) * half, first_diffraction, 0)
        if part == 2:
            hear(2)
        for step in steps:
            column_copy(group, index, step, first, count).start()
    mine = [
        pltpu.make_async_copy(
            sbuf.at[group, me], rbuf.at[group, pl.ds(pl.multiple_of(me * TL, TL), TL), :], local_sem.at[group]
        )
        for group in range(2)
    ]
    for copy in mine:
        copy.start()

    load_f.wait()
    load_s.wait()
    turn = dens[0:1, NY:]
    sine, cosine = sincos(turn)
    pair = jnp.concatenate([cosine, sine] * 4, axis=0) * (1.0 / NT)
    by_cos = jnp.dot(pair, fbuf[0], precision=lax.Precision.HIGHEST, preferred_element_type=F32)
    by_sin = jnp.dot(pair, fbuf[1], precision=lax.Precision.HIGHEST, preferred_element_type=F32)
    rows16 = lax.broadcasted_iota(jnp.int32, (16, NT), 0)
    for part, line in enumerate((by_cos[0:1] - by_sin[1:2], by_sin[0:1] + by_cos[1:2])):
        base = jnp.broadcast_to(line, (16, NT))
        for bit in range(4):
            base = jnp.where((rows16 >> bit) & 1 == 1, pltpu.roll(base, 1 << bit, axis=1), base)
        for block in range(NT // 16):
            high, low = split(pltpu.roll(base, 16 * block, axis=1) if block else base)
            for k in range(NT // 128):
                ch[k, 16 * block : 16 * block + 16, part * 128 : (part + 1) * 128] = high[:, k * 128 : (k + 1) * 128]
                cl[k, 16 * block : 16 * block + 16, part * 128 : (part + 1) * 128] = low[:, k * 128 : (k + 1) * 128]

    def tri_rows(block, carry):
        first = pl.multiple_of(block * 16, 16)
        row = lax.broadcasted_iota(jnp.int32, (16, NT), 0) + first
        col = lax.broadcasted_iota(jnp.int32, (16, NT), 1)
        tri[pl.ds(first, 16), :] = jnp.where(row < col, 1.0, 0.0).astype(BF16)
        return carry

    lax.fori_loop(0, NT // 16, tri_rows, 0)
    lane = lax.broadcasted_iota(jnp.int32, (YC, NY), 1)
    row = lax.broadcasted_iota(jnp.int32, (YC, NY), 0)
    wanted = lane == row + me * YC
    for x in range(XR):
        line = jnp.broadcast_to(dens[x : x + 1, :NY], (YC, NY))
        column = jnp.sum(jnp.where(wanted, line, 0.0), axis=1, keepdims=True)
        dcol[x * YC : (x + 1) * YC, :] = jnp.broadcast_to(column * (ionize_gain / NT), (YC, NT))
    load_w.wait()

    def kick(group):
        def rates(x, carry):
            first = pl.multiple_of(x * PAIR, PAIR)
            place = pl.ds(pl.multiple_of(x * YC, YC), YC)
            re = grid[pl.ds(first, YC), :]
            im = grid[pl.ds(first + YC, YC), :]
            intensity = re * re + im * im
            inten[place, :] = intensity
            high, low = split(dcol[place, :] * intensity * intensity)
            rh[place, :] = high
            rl[place, :] = low
            return carry

        lax.fori_loop(group * HALO, (group + 1) * HALO, rates, 0, unroll=True)
        cells = slice(group * CELLS // 2, (group + 1) * CELLS // 2)
        both = dot(jnp.concatenate([rh[cells, :], rl[cells, :]], axis=0), tri[...])
        plasma[cells, :] = both[: CELLS // 2] + both[CELLS // 2 :]

        def turn(x, carry):
            first = pl.multiple_of(x * PAIR, PAIR)
            place = pl.ds(pl.multiple_of(x * YC, YC), YC)
            re = grid[pl.ds(first, YC), :]
            im = grid[pl.ds(first + YC, YC), :]
            earlier = plasma[place, :]
            sine, cosine = sincos(kerr_gain * inten[place, :] - plasma_gain * earlier)
            amplitude = jnp.exp(-absorb_gain * earlier)
            sine = sine * amplitude
            cosine = cosine * amplitude
            high, low = split(re * cosine - im * sine)
            uh[pl.ds(first, YC), :] = high
            ul[pl.ds(first, YC), :] = low
            high, low = split(re * sine + im * cosine)
            uh[pl.ds(first + YC, YC), :] = high
            ul[pl.ds(first + YC, YC), :] = low
            return carry

        lax.fori_loop(group * HALO, (group + 1) * HALO, turn, 0, unroll=True)

    def disperse(group, chunk):
        rows = slice(group * OWN // 2, (group + 1) * OWN // 2)
        both = dot(jnp.concatenate([uh[rows, :], ul[rows, :]], axis=0), ch[chunk])
        value = both[: OWN // 2] + both[OWN // 2 :] + dot(uh[rows, :], cl[chunk])
        result = []
        for x in range(HALO):
            re = value[x * PAIR : x * PAIR + YC]
            im = value[x * PAIR + YC : (x + 1) * PAIR]
            result.append(re[:, :128] - im[:, 128:])
            result.append(re[:, 128:] + im[:, :128])
        return jnp.concatenate(result, axis=0)

    def halo_copy(index, source, first, dx, dz):
        return pltpu.make_async_remote_copy(
            src_ref=source,
            dst_ref=ext.at[pl.ds(first, source.shape[0]), :],
            send_sem=hsend.at[index],
            recv_sem=hrecv.at[index],
            device_id=(ring(dz), side(dx)),
            device_id_type=MESH,
        )

    def halo_copies(group):
        rows = pl.ds(group * 32, 32)
        towards = 2 * group - 1
        end = pl.ds(40 * group, 24)
        return [
            halo_copy(5 * group, ext.at[pl.ds(group * OWN // 2, OWN // 2), :], UP if group else DOWN, towards, 0),
            halo_copy(5 * group + 1, yhi.at[rows, :], LEFT + 32 * group, 0, 1),
            halo_copy(5 * group + 2, ylo.at[rows, :], RIGHT + 32 * group, 0, -1),
            halo_copy(5 * group + 3, yhi.at[end, :], (UP if group else DOWN) + HALO * PAIR, towards, 1),
            halo_copy(5 * group + 4, ylo.at[end, :], (UP if group else DOWN) + HALO * PAIR + 24, towards, -1),
        ]

    def split_rows(block, carry):
        place = pl.ds(pl.multiple_of(block * 16, 16), 16)
        high, low = split(ext[place, :])
        exth[place, :] = high
        extl[place, :] = low
        return carry

    low4 = lax.broadcasted_iota(jnp.int32, (8, NT), 0) < HALO
    for group in range(2):
        mine[group].wait()
        for g, index, first, count, steps in messages:
            if g == group:
                for step in steps:
                    column_copy(g, index, step, first, count).wait_recv()
        base = group * OWN // 2
        grid[base : base + OWN // 2, :] = rbuf[group].T
        kick(group)
        for chunk in range(NT // 128):
            ext[base : base + OWN // 2, chunk * 128 : (chunk + 1) * 128] = disperse(group, chunk)
        halo_copies(group)[0].start()
        for x in range(group * HALO, (group + 1) * HALO):
            first = x * PAIR
            ylo[8 * x : 8 * x + 8, :] = jnp.where(
                low4, ext[first : first + 8, :], pltpu.roll(ext[first + 16 : first + 24, :], 4, axis=0)
            )
            yhi[8 * x : 8 * x + 8, :] = jnp.where(
                low4, pltpu.roll(ext[first + 8 : first + 16, :], 4, axis=0), ext[first + 24 : first + 32, :]
            )
        for copy in halo_copies(group)[1:]:
            copy.start()

    lax.fori_loop(0, OWN // 16, split_rows, 0)
    both = dot(jnp.concatenate([wbuf[0, :, :OWN], wbuf[1, :, :OWN]], axis=0), exth[:OWN])
    grid[...] = both[:OWN] + both[OWN:] + dot(wbuf[0, :, :OWN], extl[:OWN])

    def shard_copy(group, step):
        peer = ring(step)
        return pltpu.make_async_remote_copy(
            src_ref=fin.at[group, pl.ds(pl.multiple_of(peer * TL, TL), TL), :],
            dst_ref=obuf.at[group, me],
            send_sem=bsend.at[group, step],
            recv_sem=brecv.at[group, step],
            device_id=(peer, gx),
            device_id_type=MESH,
        )

    mine = [
        pltpu.make_async_copy(
            fin.at[group, pl.ds(pl.multiple_of(me * TL, TL), TL), :], obuf.at[group, me], local_sem.at[group]
        )
        for group in range(2)
    ]
    for group in (1, 0):
        for index in (1, 2) if group else ():
            for g in range(2):
                halo_copies(g)[index].wait_recv()
        for index in (0, 3, 4):
            halo_copies(1 - group)[index].wait_recv()
        rows = slice(group * OWN // 2, (group + 1) * OWN // 2)
        first = OWN if group else UP
        lax.fori_loop(first // 16, (first + (UP - OWN if group else EXT - UP)) // 16, split_rows, 0)
        if group:
            grid[rows, :] += triple(wbuf[0, rows, OWN:UP], wbuf[1, rows, OWN:UP], exth[OWN:UP], extl[OWN:UP])
        else:
            for a, b in ((OWN, DOWN), (UP, EXT)):
                grid[rows, :] += triple(wbuf[0, rows, a:b], wbuf[1, rows, a:b], exth[a:b], extl[a:b])
        kick(group)
        for apart in (2, 1, 3, 0):
            chunk = lax.rem(lax.div(me, 4) + apart, 4)
            fin[group, pl.ds(pl.multiple_of(chunk * 128, 128), 128), :] = disperse(group, chunk).T
            for r in range(4):
                step = lax.rem(chunk * 4 + r - me + NZ, NZ)
                if apart:
                    shard_copy(group, step).start()
                else:

                    @pl.when(step != 0)
                    def _():
                        shard_copy(group, step).start()

        mine[group].start()

    for q in range(TL // TC):
        for copy in row_copies(q):
            copy.wait_send()
    for group, index, first, count, steps in messages:
        for step in steps:
            column_copy(group, index, step, first, count).wait_send()
    for group in range(2):
        for copy in halo_copies(group):
            copy.wait_send()

    slot = lax.broadcasted_iota(jnp.int32, (TL, 128), 1) // YC
    for group in (1, 0):
        mine[group].wait()
        for step in order:
            shard_copy(group, step).wait_recv()
        for h in range(2):
            turned = []
            for jj in range(8):
                part = obuf[group, h * 8 + jj]
                turned.append(pltpu.roll(part, YC * jj, axis=1) if jj else part)
            for s in range(8):
                piece = turned[0]
                for jj in range(1, 8):
                    piece = jnp.where(slot == (jj + s) % 8, turned[jj], piece)
                if s:
                    piece = pltpu.roll(piece, 128 - YC * s, axis=1)
                stage[h, pl.ds((s % 2) * TL * XR + group * HALO + s // 2, TL, stride=XR), :] = piece
    for h in range(2):
        out[:, h * 128 : (h + 1) * 128] = stage[h]
    for group in range(2):
        for step in order:
            shard_copy(group, step).wait_send()


def per_device(envelope, density_map, disp_phase):
    rows = 2 * TL * XR
    vmem = pl.BlockSpec(memory_space=pltpu.VMEM)
    anywhere = pl.BlockSpec(memory_space=pltpu.HBM)
    dma = pltpu.SemaphoreType.DMA
    result = pl.pallas_call(
        kernel,
        out_shape=jax.ShapeDtypeStruct((rows, NY), F32),
        in_specs=[anywhere] * 4,
        out_specs=vmem,
        scratch_shapes=[
            pltpu.VMEM((XR, NY + NT), F32),
            pltpu.VMEM((2, rows, 128), F32),
            pltpu.VMEM((XR + 2 * HALO, 2, TL, NY), F32),
            pltpu.VMEM((2, NZ, TL, 128), F32),
            pltpu.VMEM((2, NT, 128), F32),
            pltpu.VMEM((EXT, NT), F32),
            pltpu.VMEM((EXT, NT), BF16),
            pltpu.VMEM((EXT, NT), BF16),
            pltpu.VMEM((8 * XR, NT), F32),
            pltpu.VMEM((8 * XR, NT), F32),
            pltpu.VMEM((NT // 128, NT, 256), BF16),
            pltpu.VMEM((NT // 128, NT, 256), BF16),
            pltpu.VMEM((NT, NT), BF16),
            pltpu.VMEM((2, OWN, EXT), BF16),
            pltpu.VMEM((2, NT, NT), F32),
            pltpu.VMEM((CELLS, NT), F32),
            pltpu.VMEM((OWN, NT), F32),
            pltpu.VMEM((CELLS, NT), F32),
            pltpu.VMEM((CELLS, NT), BF16),
            pltpu.VMEM((CELLS, NT), BF16),
            pltpu.VMEM((CELLS, NT), F32),
            pltpu.VMEM((OWN, NT), BF16),
            pltpu.VMEM((OWN, NT), BF16),
            pltpu.VMEM((2, NT, 128), F32),
            pltpu.VMEM((2, NZ, TL, 128), F32),
            pltpu.SemaphoreType.REGULAR((3,)),
            dma((8,)),
            dma((TL // TC, 2)),
            dma((TL // TC, 2)),
            dma((3, NZ)),
            dma((3, NZ)),
            dma((10,)),
            dma((10,)),
            dma((2, NZ)),
            dma((2, NZ)),
        ],
        compiler_params=pltpu.CompilerParams(
            collective_id=0, has_side_effects=True, vmem_limit_bytes=53 * 1024 * 1024
        ),
        name="filament",
    )(
        envelope.reshape(rows, NY),
        jnp.concatenate([density_map, jnp.broadcast_to(disp_phase.reshape(1, NT), (XR, NT))], axis=1),
        jnp.asarray(diffraction_matrices()),
        jnp.asarray(fourier_matrices()),
    )
    return result.reshape(2, TL, XR, NY)


def solution(mesh):
    placed = (P(None, "ta", "gx", None), P("gx", None), P())
    return jax.shard_map(
        per_device, mesh=mesh, in_specs=placed, out_specs=P(None, "ta", "gx", None), check_vma=False
    )
```
